256 devices in a mesh: outer: 8 (over y, core), rep: 32 (over x, z).
Axes of the slice: x: 4, y: 4, z: 8, core: 2. Of those that a mesh axis runs over, the one named last changes fastest.
Arguments:
- gradients: bfloat16 [8, 4096, 14336], P('outer', 'rep'), may hold values from -12 to 12
- residual: bfloat16 [8, 4096, 14336], P('outer', 'rep'), may hold values from -3 to 3
- sketch: bfloat16 [32, 14336], replicated, may hold values from -0.046875 to 0.046875
Outputs:
- left_basis: float32 [32, 4096], P(None, 'rep')
- right_factor: float32 [32, 14336], P(None, 'rep')
- new_residual: bfloat16 [8, 4096, 14336], P('outer', 'rep')
The draws below stay inside these ranges and needn't reach their ends.
All inputs are finite; a program needn't handle non-finite values.
Results may differ from the reference program's by a relative error of at most 0.001.
Values sent between devices are 32-bit elements; how exact they have to be, the bound alone decides.
No kernel may reach another device: no remote copies, remote signals or barrier semaphores. Data moves between devices by JAX's collectives and lax.ppermute only.
A program may use at most 64 MiB of HBM per device.

```python
import jax
import jax.numpy as jnp
from jax import lax

D = 4096
FF = 14336
RANK = 32
N_OUTER = 8


def draw_gradients(key, part):
    key = jax.random.fold_in(key, 11)
    key_left, key_right, key_weight, key_noise = jax.random.split(key, 4)
    components = 64
    left_part = jax.random.normal(key_left, (D, components), jnp.float32)
    right_part = jax.random.normal(key_right, (components, FF), jnp.float32)
    decay = 0.1 ** (jnp.arange(components, dtype=jnp.float32) / (components - 1))
    weights = decay * jax.random.uniform(key_weight, (components,), jnp.float32, 0.7, 1.3)
    common = jnp.dot(left_part * weights, right_part) / jnp.sqrt(jnp.sum(weights * weights))
    noise = jax.random.normal(key_noise, (N_OUTER, D, FF), jnp.float32) * 0.6
    return jnp.clip(common[None] + noise, -12.0, 12.0).astype(jnp.bfloat16)


def level_of(key, dims, cuts, low, top_value):
    def one(dim, shards_of):
        heights = jax.random.uniform(jax.random.fold_in(jax.random.fold_in(key, 6), dim), (shards_of,), jnp.float32, low / len(cuts), top_value / len(cuts))
        return jnp.repeat(jnp.exp(heights), dims[dim] // shards_of).reshape((-1,) + (1,) * (len(dims) - dim - 1))

    factor_of = one(*cuts[0])
    for cut in cuts[1:]:
        factor_of = factor_of * one(*cut)
    return factor_of


def normal_values(stream_key, extent, width, limit, cuts=(), kind=jnp.bfloat16):
    array = jax.random.normal(stream_key, extent, jnp.float32) * width
    if len(cuts) > 0:
        array = level_of(stream_key, extent, cuts, -0.22, 0.18) * array
    return jnp.clip(array, min=-limit, max=limit).astype(kind)


def setup_inputs(seed: int = 0) -> dict:
    key_list = jax.random.split(jax.random.key(seed), 4)
    gradients = draw_gradients(jax.random.fold_in(key_list[3], 71), 0)
    residual = normal_values(key_list[1], (N_OUTER, D, FF), 0.5, 3.0, ((0, 8), (1, 32)))
    sketch = normal_values(key_list[2], (RANK, FF), FF ** -0.5, 0.046875)
    return {"gradients": gradients, "residual": residual, "sketch": sketch}


def merge_pair(grad_block, memory_block):
    return grad_block.astype(jnp.float32) + memory_block.astype(jnp.float32)

def reference(gradients, residual, sketch):
    probe_rows = sketch.astype(jnp.float32)

    def left_step(accum, pair):
        merged = merge_pair(pair[0], pair[1])
        term = lax.dot_general(probe_rows, merged, (((1,), (1,)), ((), ())), precision=lax.Precision.HIGHEST)
        return (accum + term, None)
    summed, _ = lax.scan(left_step, jnp.zeros((RANK, D), jnp.float32), (gradients, residual))
    summed = summed / N_OUTER
    gram_matrix = jnp.dot(summed, summed.T, precision=lax.Precision.HIGHEST)
    lower_factor = jnp.linalg.cholesky(gram_matrix)
    left_basis = jax.scipy.linalg.solve_triangular(lower_factor, summed, lower=True)

    def right_step(accum, pair):
        merged = merge_pair(pair[0], pair[1])
        return (accum + jnp.dot(left_basis, merged, precision=lax.Precision.HIGHEST), None)
    right_factor, _ = lax.scan(right_step, jnp.zeros((RANK, FF), jnp.float32), (gradients, residual))
    right_factor = right_factor / N_OUTER
    update = lax.dot_general(left_basis, right_factor, (((0,), (0,)), ((), ())), precision=lax.Precision.HIGHEST)

    def residual_step(pair):
        return (merge_pair(pair[0], pair[1]) - update).astype(jnp.bfloat16)
    new_residual = lax.map(residual_step, (gradients, residual))
    return (left_basis, right_factor, new_residual)
```

```python
import jax
import jax.numpy as jnp
from jax import lax
from jax.experimental import pallas as pl
from jax.experimental.pallas import tpu as pltpu
from jax.sharding import Mesh
from jax.sharding import PartitionSpec as P

AXES = ("y", "c", "x", "z4", "z2", "z1")
SIZES = (4, 2, 4, 2, 2, 2)
SPREAD = ("y", "x", "z1")
ROWS = 128
FF = 14336
RANK = 32
CHUNKS = 16
WIDTH = FF // CHUNKS
TILES = WIDTH // 128
LOADS = 8
LOAD_WIDTH = FF // LOADS
F32 = jnp.float32
BF16 = jnp.bfloat16
MB = 1024 * 1024

ANY = pl.BlockSpec(memory_space=pl.ANY)
VMEM = pl.BlockSpec(memory_space=pltpu.VMEM)
SMEM = pl.BlockSpec(memory_space=pltpu.SMEM)


def params(limit):
    return pltpu.CompilerParams(vmem_limit_bytes=limit)


def three_parts(value):
    first = value.astype(BF16).astype(F32)
    rest = value - first
    second = rest.astype(BF16).astype(F32)
    return first, second, rest - second


def sketch_kernel(grad_hbm, memory_hbm, sketch_hbm, out_ref, grad_ref, memory_ref, sketch_ref, sems):
    copies = []
    for step in range(LOADS):
        cols = pl.ds(step * LOAD_WIDTH, LOAD_WIDTH)
        group = [
            pltpu.make_async_copy(src.at[:, cols], dst.at[:, cols], sems.at[step, which])
            for which, (src, dst) in enumerate(
                ((sketch_hbm, sketch_ref), (grad_hbm, grad_ref), (memory_hbm, memory_ref))
            )
        ]
        for copy in group:
            copy.start()
        copies.append(group)
    total = jnp.zeros((RANK, ROWS), F32)
    for step in range(LOADS):
        for copy in copies[step]:
            copy.wait()
        cols = pl.ds(step * LOAD_WIDTH, LOAD_WIDTH)
        probe = sketch_ref[:, cols]
        for block in (grad_ref, memory_ref):
            total += lax.dot_general(
                probe, block[:, cols], (((1,), (1,)), ((), ())), preferred_element_type=F32
            )
    out_ref[...] = total


def left_sketch(grad, memory, sketch):
    return pl.pallas_call(
        sketch_kernel,
        out_shape=(
            jax.ShapeDtypeStruct((RANK, ROWS), F32),
            pltpu.VMEM((ROWS, FF), BF16),
            pltpu.VMEM((ROWS, FF), BF16),
        ),
        in_specs=[ANY, ANY, ANY],
        out_specs=(VMEM, VMEM, VMEM),
        scratch_shapes=[pltpu.VMEM((RANK, FF), BF16), pltpu.SemaphoreType.DMA((LOADS, 3))],
        compiler_params=params(16 * MB),
        name="left_sketch",
    )(grad, memory, sketch)


def project_kernel(ids_ref, parts_ref, grad_ref, memory_ref, own_ref, other_ref):
    core = ids_ref[0]
    summed = ((parts_ref[0] + parts_ref[1]) + (parts_ref[2] + parts_ref[3])) * (1.0 / 8)
    tiled = jnp.concatenate([summed] * 4, axis=0)
    square = lax.dot_general(
        summed, tiled, (((1,), (1,)), ((), ())), precision=lax.Precision.HIGHEST, preferred_element_type=F32
    )
    lane = lax.broadcasted_iota(jnp.int32, (8, 128), 1) // 32
    gram = jnp.zeros((8, 128), F32)
    for group in range(4):
        gram = jnp.where(lane == group, square[8 * group : 8 * group + 8], gram)
    groups = [summed[8 * q : 8 * q + 8] for q in range(4)]
    even = core == 0
    ordered = jnp.concatenate(
        [
            jnp.where(even, groups[0], groups[1]),
            jnp.where(even, groups[2], groups[3]),
            jnp.where(even, groups[1], groups[0]),
            jnp.where(even, groups[3], groups[2]),
        ],
        axis=0,
    )
    left = jnp.concatenate(three_parts(ordered), axis=0).astype(BF16)
    left = jnp.concatenate([left, left], axis=1)

    @pl.loop(0, CHUNKS)
    def _(chunk):
        cols = pl.ds(pl.multiple_of(chunk * WIDTH, 128), WIDTH)
        both = jnp.concatenate([grad_ref[:, cols], memory_ref[:, cols]], axis=0)
        product = jnp.dot(left, both, preferred_element_type=F32)
        product = product[:32] + (product[32:64] + product[64:])
        for half, ref in enumerate((own_ref, other_ref)):
            for row in range(2):
                base = 16 * half + 8 * row
                for tile in range(TILES):
                    ref[chunk, row, tile] = product[base : base + 8, 128 * tile : 128 * tile + 128]
                ref[chunk, row, TILES] = gram


def project(ids, parts, grad, memory):
    shape = jax.ShapeDtypeStruct((CHUNKS, 2, TILES + 1, 8, 128), F32)
    return pl.pallas_call(
        project_kernel,
        out_shape=(shape, shape),
        in_specs=[SMEM, VMEM, VMEM, VMEM],
        out_specs=(VMEM, VMEM),
        compiler_params=params(24 * MB),
        name="project",
    )(ids, parts, grad, memory)


def factor_kernel(ids_ref, gram_ref, parts_ref, left_ref, inverse_ref, back_ref):
    core = ids_ref[0]
    rows = lax.broadcasted_iota(jnp.int32, (RANK, 128), 0)
    lanes = lax.broadcasted_iota(jnp.int32, (RANK, 128), 1)
    tile = gram_ref[...] * (1.0 / 8)
    packed = jnp.concatenate([tile] + [pltpu.roll(tile, 128 - 32 * q, 1) for q in (1, 2, 3)], axis=0)
    work = jnp.where(lanes < 32, packed, jnp.where(lanes == rows + 32, 1.0, 0.0))
    basis = ((parts_ref[0] + parts_ref[1]) + (parts_ref[2] + parts_ref[3])) * (1.0 / 8)
    scale = jnp.ones((RANK, 128), F32)
    for step in range(RANK):
        column = jnp.broadcast_to(work[:, step : step + 1], (RANK, 128))
        pivot = column[step : step + 1]
        scale = jnp.where(rows == step, pivot, scale)
        factor = jnp.where(rows > step, column / pivot, 0.0)
        work = work - factor * work[step : step + 1]
        basis = basis - factor * basis[step : step + 1]
    scale = lax.rsqrt(scale)
    left = basis * scale
    left_ref[...] = left
    inverse = pltpu.roll(work * scale, 96, 1)
    inverse = jnp.where(lanes < 32, inverse, 0.0)
    inverse_ref[...] = inverse
    solved = lax.dot_general(
        inverse, left, (((0,), (0,)), ((), ())), precision=lax.Precision.HIGHEST, preferred_element_type=F32
    )[:32] * (1.0 / 8)
    even = core == 0
    groups = [solved[8 * q : 8 * q + 8] for q in range(4)]
    ordered = jnp.concatenate(
        [
            jnp.where(even, groups[0], groups[1]),
            jnp.where(even, groups[2], groups[3]),
            jnp.where(even, groups[1], groups[0]),
            jnp.where(even, groups[3], groups[2]),
        ],
        axis=0,
    )
    one, two, three = three_parts(ordered)
    stack = jnp.concatenate([one, two, three, one, two, one, jnp.zeros((64, 128), F32)], axis=0)
    back_ref[...] = stack.T.astype(BF16)


def factor(ids, gram, parts):
    return pl.pallas_call(
        factor_kernel,
        out_shape=(
            jax.ShapeDtypeStruct((RANK, ROWS), F32),
            jax.ShapeDtypeStruct((RANK, 128), F32),
            jax.ShapeDtypeStruct((ROWS, 256), BF16),
        ),
        in_specs=[SMEM, VMEM, VMEM],
        out_specs=(VMEM, VMEM, VMEM),
        compiler_params=params(8 * MB),
        cost_estimate=pl.CostEstimate(flops=10**6, bytes_accessed=10**6, transcendentals=0),
        name="factor",
    )(ids, gram, parts)


def update_kernel(ids_ref, own_ref, other_ref, inverse_ref, back_ref, grad_ref, memory_ref, share_ref, out_hbm, out_ref, sems):
    even = ids_ref[0] == 0
    back = back_ref[:, :192]

    def block(chunk, tile):
        parts = [ref[chunk, row, tile] for ref in (own_ref, other_ref) for row in range(2)]
        return jnp.concatenate(parts, axis=0)

    @pl.loop(0, CHUNKS)
    def _(chunk):
        cols = pl.ds(pl.multiple_of(chunk * WIDTH, 128), WIDTH)
        right = jnp.concatenate([block(chunk, tile) for tile in range(TILES)], axis=1)
        one, two, three = (part.astype(BF16) for part in three_parts(right))
        stack = jnp.concatenate([one, one, one, two, two, three], axis=0)
        update = jnp.dot(back, stack, preferred_element_type=F32)
        merged = grad_ref[:, cols].astype(F32) + memory_ref[:, cols].astype(F32)
        out_ref[:, cols] = (merged - update).astype(BF16)
        pltpu.make_async_copy(out_ref.at[:, cols], out_hbm.at[:, cols], sems.at[chunk]).start()

    mine, odd = ids_ref[1], ids_ref[2]

    def natural(tile):
        own0, own1, other0, other1 = (ref[mine, row, tile] for ref in (own_ref, other_ref) for row in range(2))
        return jnp.concatenate(
            [
                jnp.where(even, own0, other0),
                jnp.where(even, other0, own0),
                jnp.where(even, own1, other1),
                jnp.where(even, other1, own1),
            ],
            axis=0,
        )

    right = jnp.concatenate([natural(tile) for tile in range(TILES)], axis=1)
    share = jnp.dot(
        inverse_ref[:, :32], right, precision=lax.Precision.HIGHEST, preferred_element_type=F32
    ) * (1.0 / 8)
    half = WIDTH // 2
    share_ref[...] = jnp.where(odd == 0, share[:, :half], share[:, half:])

    for chunk in range(CHUNKS):
        cols = pl.ds(chunk * WIDTH, WIDTH)
        pltpu.make_async_copy(out_ref.at[:, cols], out_hbm.at[:, cols], sems.at[chunk]).wait()


def finish(ids, own, other, inverse, back, grad, memory):
    return pl.pallas_call(
        update_kernel,
        out_shape=(
            jax.ShapeDtypeStruct((RANK, WIDTH // 2), F32),
            jax.ShapeDtypeStruct((ROWS, FF), BF16),
        ),
        in_specs=[SMEM] + [VMEM] * 6,
        out_specs=(VMEM, ANY),
        scratch_shapes=[pltpu.VMEM((ROWS, FF), BF16), pltpu.SemaphoreType.DMA((CHUNKS,))],
        compiler_params=params(24 * MB),
        name="finish",
    )(ids, own, other, inverse, back, grad, memory)


def exchange(value, axes):
    return lax.all_to_all(value, axes, 0, 0, tiled=True)


def swap(value):
    return lax.ppermute(value, "c", [(0, 1), (1, 0)])


def spread(value, axes, count):
    return exchange(jnp.broadcast_to(value[None], (count,) + value.shape), axes)


def resident(value):
    return pltpu.with_memory_space_constraint(value, pltpu.VMEM)


def on_device(gradients, residual, sketch):
    core = lax.axis_index("c")
    block = lax.axis_index(("x", "z4", "z2"))
    ids = jnp.stack([core, block, lax.axis_index("z1")]).astype(jnp.int32)
    partial, grad, memory = left_sketch(gradients[0], residual[0], sketch)
    pair = partial + swap(partial)
    parts = spread(pair, "y", 4)
    own, other = project(ids, parts, resident(grad), resident(memory))
    terms = own + swap(other)
    terms = exchange(terms.reshape(32, TILES + 1, 8, 128), SPREAD)
    terms = jnp.sum(terms, axis=0)
    terms = jnp.sum(spread(terms, ("z4", "z2"), 4).reshape((4,) + terms.shape), axis=0)
    gathered = spread(terms[:TILES], SPREAD, 32).reshape(CHUNKS, 2, TILES, 8, 128)
    gathered_other = swap(gathered)
    left, inverse, back = factor(ids, terms[TILES], parts)
    share, fresh = finish(ids, gathered, gathered_other, inverse, back, resident(grad), resident(memory))
    return left, share, fresh[None]


def solution(mesh):
    fine = Mesh(mesh.devices.reshape(SIZES), AXES)
    outer, rep = ("y", "c"), ("x", "z4", "z2", "z1")
    return jax.shard_map(
        on_device,
        mesh=fine,
        in_specs=(P(outer, rep, None), P(outer, rep, None), P()),
        out_specs=(P(None, rep), P(None, rep), P(outer, rep, None)),
        check_vma=False,
    )
```

```python
import jax
import jax.numpy as jnp
from jax import lax
from jax.experimental import pallas as pl
from jax.experimental.pallas import tpu as pltpu
from jax.sharding import Mesh
from jax.sharding import PartitionSpec as P

AXES = ("y", "c", "x", "z4", "z2", "z1")
SIZES = (4, 2, 4, 2, 2, 2)
SPREAD = ("y", "x", "z1")
ROWS = 128
FF = 14336
RANK = 32
CHUNKS = 16
WIDTH = FF // CHUNKS
TILES = WIDTH // 128
LOADS = 8
LOAD_WIDTH = FF // LOADS
F32 = jnp.float32
BF16 = jnp.bfloat16
MB = 1024 * 1024

ANY = pl.BlockSpec(memory_space=pl.ANY)
VMEM = pl.BlockSpec(memory_space=pltpu.VMEM)
SMEM = pl.BlockSpec(memory_space=pltpu.SMEM)
BLOCKS = [pltpu.VMEM((ROWS, FF), BF16), pltpu.VMEM((ROWS, FF), BF16), pltpu.SemaphoreType.DMA((CHUNKS, 2))]


def params(limit):
    return pltpu.CompilerParams(vmem_limit_bytes=limit)


def three_parts(value):
    first = value.astype(BF16).astype(F32)
    rest = value - first
    second = rest.astype(BF16).astype(F32)
    return first, second, rest - second


def loads(grad_hbm, memory_hbm, grad_ref, memory_ref, sems):
    def copies(chunk):
        cols = pl.ds(pl.multiple_of(chunk * WIDTH, 128), WIDTH)
        return (
            pltpu.make_async_copy(grad_hbm.at[:, cols], grad_ref.at[:, cols], sems.at[chunk, 0]),
            pltpu.make_async_copy(memory_hbm.at[:, cols], memory_ref.at[:, cols], sems.at[chunk, 1]),
        )

    return copies


def sketch_kernel(grad_hbm, memory_hbm, sketch_hbm, out_ref, grad_ref, memory_ref, sketch_ref, sems):
    copies = []
    for step in range(LOADS):
        cols = pl.ds(step * LOAD_WIDTH, LOAD_WIDTH)
        group = [
            pltpu.make_async_copy(src.at[:, cols], dst.at[:, cols], sems.at[step, which])
            for which, (src, dst) in enumerate(
                ((sketch_hbm, sketch_ref), (grad_hbm, grad_ref), (memory_hbm, memory_ref))
            )
        ]
        for copy in group:
            copy.start()
        copies.append(group)
    total = jnp.zeros((RANK, ROWS), F32)
    for step in range(LOADS):
        for copy in copies[step]:
            copy.wait()
        cols = pl.ds(step * LOAD_WIDTH, LOAD_WIDTH)
        probe = sketch_ref[:, cols]
        for block in (grad_ref, memory_ref):
            total += lax.dot_general(
                probe, block[:, cols], (((1,), (1,)), ((), ())), preferred_element_type=F32
            )
    out_ref[...] = total


def left_sketch(grad, memory, sketch):
    return pl.pallas_call(
        sketch_kernel,
        out_shape=jax.ShapeDtypeStruct((RANK, ROWS), F32),
        in_specs=[ANY, ANY, ANY],
        out_specs=VMEM,
        scratch_shapes=[
            pltpu.VMEM((ROWS, FF), BF16),
            pltpu.VMEM((ROWS, FF), BF16),
            pltpu.VMEM((RANK, FF), BF16),
            pltpu.SemaphoreType.DMA((LOADS, 3)),
        ],
        compiler_params=params(24 * MB),
        name="left_sketch",
    )(grad, memory, sketch)


def project_kernel(ids_ref, parts_ref, grad_hbm, memory_hbm, own_ref, other_ref, grad_ref, memory_ref, sems):
    copies = loads(grad_hbm, memory_hbm, grad_ref, memory_ref, sems)
    for chunk in range(CHUNKS):
        for copy in copies(chunk):
            copy.start()
    core = ids_ref[0]
    summed = ((parts_ref[0] + parts_ref[1]) + (parts_ref[2] + parts_ref[3])) * (1.0 / 8)
    tiled = jnp.concatenate([summed] * 4, axis=0)
    square = lax.dot_general(
        summed, tiled, (((1,), (1,)), ((), ())), precision=lax.Precision.HIGHEST, preferred_element_type=F32
    )
    lane = lax.broadcasted_iota(jnp.int32, (8, 128), 1) // 32
    gram = jnp.zeros((8, 128), F32)
    for group in range(4):
        gram = jnp.where(lane == group, square[8 * group : 8 * group + 8], gram)
    groups = [summed[8 * q : 8 * q + 8] for q in range(4)]
    even = core == 0
    ordered = jnp.concatenate(
        [
            jnp.where(even, groups[0], groups[1]),
            jnp.where(even, groups[2], groups[3]),
            jnp.where(even, groups[1], groups[0]),
            jnp.where(even, groups[3], groups[2]),
        ],
        axis=0,
    )
    left = jnp.concatenate(three_parts(ordered), axis=0).astype(BF16)
    left = jnp.concatenate([left, left], axis=1)

    @pl.loop(0, CHUNKS)
    def _(chunk):
        for copy in copies(chunk):
            copy.wait()
        cols = pl.ds(pl.multiple_of(chunk * WIDTH, 128), WIDTH)
        both = jnp.concatenate([grad_ref[:, cols], memory_ref[:, cols]], axis=0)
        product = jnp.dot(left, both, preferred_element_type=F32)
        product = product[:32] + (product[32:64] + product[64:])
        for half, ref in enumerate((own_ref, other_ref)):
            for row in range(2):
                base = 16 * half + 8 * row
                for tile in range(TILES):
                    ref[chunk, row, tile] = product[base : base + 8, 128 * tile : 128 * tile + 128]
                ref[chunk, row, TILES] = gram


def project(ids, parts, grad, memory):
    shape = jax.ShapeDtypeStruct((CHUNKS, 2, TILES + 1, 8, 128), F32)
    return pl.pallas_call(
        project_kernel,
        out_shape=(shape, shape),
        in_specs=[SMEM, VMEM, ANY, ANY],
        out_specs=(VMEM, VMEM),
        scratch_shapes=BLOCKS,
        compiler_params=params(24 * MB),
        name="project",
    )(ids, parts, grad, memory)


def factor_kernel(
    ids_ref, gram_ref, parts_ref, grad_hbm, memory_hbm, left_ref, inverse_ref, back_ref, grad_ref, memory_ref, sems
):
    copies = loads(grad_hbm, memory_hbm, grad_ref, memory_ref, sems)
    for chunk in range(CHUNKS):
        for copy in copies(chunk):
            copy.start()
    core = ids_ref[0]
    rows = lax.broadcasted_iota(jnp.int32, (RANK, 128), 0)
    lanes = lax.broadcasted_iota(jnp.int32, (RANK, 128), 1)
    tile = gram_ref[...] * (1.0 / 8)
    packed = jnp.concatenate([tile] + [pltpu.roll(tile, 128 - 32 * q, 1) for q in (1, 2, 3)], axis=0)
    work = jnp.where(lanes < 32, packed, jnp.where(lanes == rows + 32, 1.0, 0.0))
    basis = ((parts_ref[0] + parts_ref[1]) + (parts_ref[2] + parts_ref[3])) * (1.0 / 8)
    scale = jnp.ones((RANK, 128), F32)
    for step in range(RANK):
        column = jnp.broadcast_to(work[:, step : step + 1], (RANK, 128))
        pivot = column[step : step + 1]
        scale = jnp.where(rows == step, pivot, scale)
        factor = jnp.where(rows > step, column / pivot, 0.0)
        work = work - factor * work[step : step + 1]
        basis = basis - factor * basis[step : step + 1]
    scale = lax.rsqrt(scale)
    left = basis * scale
    left_ref[...] = left
    inverse = pltpu.roll(work * scale, 96, 1)
    inverse = jnp.where(lanes < 32, inverse, 0.0)
    inverse_ref[...] = inverse
    solved = lax.dot_general(
        inverse, left, (((0,), (0,)), ((), ())), precision=lax.Precision.HIGHEST, preferred_element_type=F32
    )[:32] * (1.0 / 8)
    even = core == 0
    groups = [solved[8 * q : 8 * q + 8] for q in range(4)]
    ordered = jnp.concatenate(
        [
            jnp.where(even, groups[0], groups[1]),
            jnp.where(even, groups[2], groups[3]),
            jnp.where(even, groups[1], groups[0]),
            jnp.where(even, groups[3], groups[2]),
        ],
        axis=0,
    )
    one, two, three = three_parts(ordered)
    stack = jnp.concatenate([one, two, three, one, two, one, jnp.zeros((64, 128), F32)], axis=0)
    back_ref[...] = stack.T.astype(BF16)
    for chunk in range(CHUNKS):
        for copy in copies(chunk):
            copy.wait()


def factor(ids, gram, parts, grad, memory):
    return pl.pallas_call(
        factor_kernel,
        out_shape=(
            jax.ShapeDtypeStruct((RANK, ROWS), F32),
            jax.ShapeDtypeStruct((RANK, 128), F32),
            jax.ShapeDtypeStruct((ROWS, 256), BF16),
            pltpu.VMEM((ROWS, FF), BF16),
            pltpu.VMEM((ROWS, FF), BF16),
        ),
        in_specs=[SMEM, VMEM, VMEM, ANY, ANY],
        out_specs=(VMEM,) * 5,
        scratch_shapes=[pltpu.SemaphoreType.DMA((CHUNKS, 2))],
        compiler_params=params(8 * MB),
        cost_estimate=pl.CostEstimate(flops=10**6, bytes_accessed=10**6, transcendentals=0),
        name="factor",
    )(ids, gram, parts, grad, memory)


def update_kernel(ids_ref, own_ref, other_ref, inverse_ref, back_ref, grad_ref, memory_ref, share_ref, out_hbm, out_ref, sems):
    even = ids_ref[0] == 0
    back = back_ref[:, :192]

    def block(chunk, tile):
        parts = [ref[chunk, row, tile] for ref in (own_ref, other_ref) for row in range(2)]
        return jnp.concatenate(parts, axis=0)

    @pl.loop(0, CHUNKS)
    def _(chunk):
        cols = pl.ds(pl.multiple_of(chunk * WIDTH, 128), WIDTH)
        right = jnp.concatenate([block(chunk, tile) for tile in range(TILES)], axis=1)
        one, two, three = (part.astype(BF16) for part in three_parts(right))
        stack = jnp.concatenate([one, one, one, two, two, three], axis=0)
        update = jnp.dot(back, stack, preferred_element_type=F32)
        merged = grad_ref[:, cols].astype(F32) + memory_ref[:, cols].astype(F32)
        out_ref[:, cols] = (merged - update).astype(BF16)
        pltpu.make_async_copy(out_ref.at[:, cols], out_hbm.at[:, cols], sems.at[chunk]).start()

    mine, odd = ids_ref[1], ids_ref[2]

    def natural(tile):
        own0, own1, other0, other1 = (ref[mine, row, tile] for ref in (own_ref, other_ref) for row in range(2))
        return jnp.concatenate(
            [
                jnp.where(even, own0, other0),
                jnp.where(even, other0, own0),
                jnp.where(even, own1, other1),
                jnp.where(even, other1, own1),
            ],
            axis=0,
        )

    right = jnp.concatenate([natural(tile) for tile in range(TILES)], axis=1)
    share = jnp.dot(
        inverse_ref[:, :32], right, precision=lax.Precision.HIGHEST, preferred_element_type=F32
    ) * (1.0 / 8)
    half = WIDTH // 2
    share_ref[...] = jnp.where(odd == 0, share[:, :half], share[:, half:])

    for chunk in range(CHUNKS):
        cols = pl.ds(chunk * WIDTH, WIDTH)
        pltpu.make_async_copy(out_ref.at[:, cols], out_hbm.at[:, cols], sems.at[chunk]).wait()


def finish(ids, own, other, inverse, back, grad, memory):
    return pl.pallas_call(
        update_kernel,
        out_shape=(
            jax.ShapeDtypeStruct((RANK, WIDTH // 2), F32),
            jax.ShapeDtypeStruct((ROWS, FF), BF16),
        ),
        in_specs=[SMEM] + [VMEM] * 6,
        out_specs=(VMEM, ANY),
        scratch_shapes=[pltpu.VMEM((ROWS, FF), BF16), pltpu.SemaphoreType.DMA((CHUNKS,))],
        compiler_params=params(24 * MB),
        name="finish",
    )(ids, own, other, inverse, back, grad, memory)


def exchange(value, axes):
    return lax.all_to_all(value, axes, 0, 0, tiled=True)


def swap(value):
    return lax.ppermute(value, "c", [(0, 1), (1, 0)])


def spread(value, axes, count):
    return exchange(jnp.broadcast_to(value[None], (count,) + value.shape), axes)


def resident(value):
    return pltpu.with_memory_space_constraint(value, pltpu.VMEM)


def far(value):
    return pltpu.with_memory_space_constraint(value, pltpu.HBM)


def on_device(gradients, residual, sketch):
    core = lax.axis_index("c")
    block = lax.axis_index(("x", "z4", "z2"))
    ids = jnp.stack([core, block, lax.axis_index("z1")]).astype(jnp.int32)
    grad, memory = far(gradients[0]), far(residual[0])
    partial = left_sketch(grad, memory, far(sketch))
    pair = partial + swap(partial)
    parts = spread(pair, "y", 4)
    own, other = project(ids, parts, grad, memory)
    terms = own + swap(other)
    terms = exchange(terms.reshape(32, TILES + 1, 8, 128), SPREAD)
    terms = jnp.sum(terms, axis=0)
    terms = jnp.sum(spread(terms, ("z4", "z2"), 4).reshape((4,) + terms.shape), axis=0)
    gathered = spread(terms[:TILES], SPREAD, 32).reshape(CHUNKS, 2, TILES, 8, 128)
    gathered_other = swap(gathered)
    left, inverse, back, near_grad, near_memory = factor(ids, terms[TILES], parts, grad, memory)
    share, fresh = finish(ids, gathered, gathered_other, inverse, back, resident(near_grad), resident(near_memory))
    return left, share, fresh[None]


def solution(mesh):
    fine = Mesh(mesh.devices.reshape(SIZES), AXES)
    outer, rep = ("y", "c"), ("x", "z4", "z2", "z1")
    return jax.shard_map(
        on_device,
        mesh=fine,
        in_specs=(P(outer, rep, None), P(outer, rep, None), P()),
        out_specs=(P(None, rep), P(None, rep), P(outer, rep, None)),
        check_vma=False,
    )
```

```python
import jax
import jax.numpy as jnp
from jax import lax
from jax.experimental import pallas as pl
from jax.experimental.pallas import tpu as pltpu
from jax.sharding import Mesh
from jax.sharding import PartitionSpec as P

AXES = ("y", "c", "x", "z4", "z2", "z1")
SIZES = (4, 2, 4, 2, 2, 2)
SPREAD = ("y", "x", "z1")
ROWS = 128
FF = 14336
RANK = 32
CHUNKS = 16
WIDTH = FF // CHUNKS
TILES = WIDTH // 128
LOADS = 8
LOAD_WIDTH = FF // LOADS
GROUP = 4
STEPS = CHUNKS // GROUP
STEP_WIDTH = GROUP * WIDTH
F32 = jnp.float32
BF16 = jnp.bfloat16
MB = 1024 * 1024

ANY = pl.BlockSpec(memory_space=pl.ANY)
VMEM = pl.BlockSpec(memory_space=pltpu.VMEM)
SMEM = pl.BlockSpec(memory_space=pltpu.SMEM)


def params(limit):
    return pltpu.CompilerParams(vmem_limit_bytes=limit)


def three_parts(value):
    first = value.astype(BF16).astype(F32)
    rest = value - first
    second = rest.astype(BF16).astype(F32)
    return first, second, rest - second


def sketch_kernel(grad_hbm, memory_hbm, sketch_hbm, out_ref, grad_ref, memory_ref, sketch_ref, sems):
    copies = []
    for step in range(LOADS):
        cols = pl.ds(step * LOAD_WIDTH, LOAD_WIDTH)
        group = [
            pltpu.make_async_copy(src.at[:, cols], dst.at[:, cols], sems.at[step, which])
            for which, (src, dst) in enumerate(
                ((sketch_hbm, sketch_ref), (grad_hbm, grad_ref), (memory_hbm, memory_ref))
            )
        ]
        for copy in group:
            copy.start()
        copies.append(group)
    total = jnp.zeros((RANK, ROWS), F32)
    for step in range(LOADS):
        for copy in copies[step]:
            copy.wait()
        cols = pl.ds(step * LOAD_WIDTH, LOAD_WIDTH)
        probe = sketch_ref[:, cols]
        for block in (grad_ref, memory_ref):
            total += lax.dot_general(
                probe, block[:, cols], (((1,), (1,)), ((), ())), preferred_element_type=F32
            )
    out_ref[...] = total


def left_sketch(grad, memory, sketch):
    return pl.pallas_call(
        sketch_kernel,
        out_shape=(
            jax.ShapeDtypeStruct((RANK, ROWS), F32),
            pltpu.VMEM((ROWS, FF), BF16),
            pltpu.VMEM((ROWS, FF), BF16),
        ),
        in_specs=[ANY, ANY, ANY],
        out_specs=(VMEM, VMEM, VMEM),
        scratch_shapes=[pltpu.VMEM((RANK, FF), BF16), pltpu.SemaphoreType.DMA((LOADS, 3))],
        compiler_params=params(16 * MB),
        name="left_sketch",
    )(grad, memory, sketch)


def mean_of(part_refs):
    one, two, three, four = (ref[...] for ref in part_refs)
    return ((one + two) + (three + four)) * (1.0 / 8)


def project_kernel(ids_ref, *refs):
    part_refs, (grad_ref, memory_ref, own_ref, other_ref) = refs[:4], refs[4:]
    core = ids_ref[0]
    summed = mean_of(part_refs)
    tiled = jnp.concatenate([summed] * 4, axis=0)
    square = lax.dot_general(
        summed, tiled, (((1,), (1,)), ((), ())), precision=lax.Precision.HIGHEST, preferred_element_type=F32
    )
    lane = lax.broadcasted_iota(jnp.int32, (8, 128), 1) // 32
    gram = jnp.zeros((8, 128), F32)
    for group in range(4):
        gram = jnp.where(lane == group, square[8 * group : 8 * group + 8], gram)
    groups = [summed[8 * q : 8 * q + 8] for q in range(4)]
    even = core == 0
    ordered = jnp.concatenate(
        [
            jnp.where(even, groups[0], groups[1]),
            jnp.where(even, groups[2], groups[3]),
            jnp.where(even, groups[1], groups[0]),
            jnp.where(even, groups[3], groups[2]),
        ],
        axis=0,
    )
    left = jnp.concatenate(three_parts(ordered), axis=0).astype(BF16)
    left = jnp.concatenate([left, left], axis=1)

    @pl.loop(0, STEPS, unroll=2)
    def _(step):
        cols = pl.ds(pl.multiple_of(step * STEP_WIDTH, 128), STEP_WIDTH)
        both = jnp.concatenate([grad_ref[:, cols], memory_ref[:, cols]], axis=0)
        product = jnp.dot(left, both, preferred_element_type=F32)
        product = product[:32] + (product[32:64] + product[64:])
        for member in range(GROUP):
            chunk = step * GROUP + member
            for half, ref in enumerate((own_ref, other_ref)):
                for row in range(2):
                    base = 16 * half + 8 * row
                    for tile in range(TILES):
                        left_edge = WIDTH * member + 128 * tile
                        ref[chunk, row, tile] = product[base : base + 8, left_edge : left_edge + 128]
                    ref[chunk, row, TILES] = gram


def project(ids, parts, grad, memory):
    shape = jax.ShapeDtypeStruct((CHUNKS, 2, TILES + 1, 8, 128), F32)
    return pl.pallas_call(
        project_kernel,
        out_shape=(shape, shape),
        in_specs=[SMEM] + [VMEM] * 6,
        out_specs=(VMEM, VMEM),
        compiler_params=params(16 * MB),
        name="project",
    )(ids, *parts, grad, memory)


def factor_kernel(ids_ref, gram_ref, *refs):
    part_refs, (left_ref, inverse_ref, back_ref) = refs[:4], refs[4:]
    core = ids_ref[0]
    rows = lax.broadcasted_iota(jnp.int32, (RANK, 128), 0)
    lanes = lax.broadcasted_iota(jnp.int32, (RANK, 128), 1)
    tile = gram_ref[...] * (1.0 / 8)
    packed = jnp.concatenate([tile] + [pltpu.roll(tile, 128 - 32 * q, 1) for q in (1, 2, 3)], axis=0)
    work = jnp.where(lanes < 32, packed, jnp.where(lanes == rows + 32, 1.0, 0.0))
    basis = mean_of(part_refs)
    scale = jnp.ones((RANK, 128), F32)
    for step in range(RANK):
        column = jnp.broadcast_to(work[:, step : step + 1], (RANK, 128))
        pivot = column[step : step + 1]
        scale = jnp.where(rows == step, pivot, scale)
        factor = jnp.where(rows > step, column / pivot, 0.0)
        work = work - factor * work[step : step + 1]
        basis = basis - factor * basis[step : step + 1]
    scale = lax.rsqrt(scale)
    left = basis * scale
    left_ref[...] = left
    inverse = pltpu.roll(work * scale, 96, 1)
    inverse = jnp.where(lanes < 32, inverse, 0.0)
    inverse_ref[...] = inverse
    solved = lax.dot_general(
        inverse, left, (((0,), (0,)), ((), ())), precision=lax.Precision.HIGHEST, preferred_element_type=F32
    )[:32] * (1.0 / 8)
    even = core == 0
    groups = [solved[8 * q : 8 * q + 8] for q in range(4)]
    ordered = jnp.concatenate(
        [
            jnp.where(even, groups[0], groups[1]),
            jnp.where(even, groups[2], groups[3]),
            jnp.where(even, groups[1], groups[0]),
            jnp.where(even, groups[3], groups[2]),
        ],
        axis=0,
    )
    one, two, three = three_parts(ordered)
    stack = jnp.concatenate([one, two, three, one, two, one, jnp.zeros((64, 128), F32)], axis=0)
    back_ref[...] = stack.T.astype(BF16)


def factor(ids, gram, parts):
    return pl.pallas_call(
        factor_kernel,
        out_shape=(
            jax.ShapeDtypeStruct((RANK, ROWS), F32),
            jax.ShapeDtypeStruct((RANK, 128), F32),
            jax.ShapeDtypeStruct((ROWS, 256), BF16),
        ),
        in_specs=[SMEM] + [VMEM] * 5,
        out_specs=(VMEM, VMEM, VMEM),
        compiler_params=params(16 * MB),
        cost_estimate=pl.CostEstimate(flops=10**9, bytes_accessed=10**7, transcendentals=0),
        name="factor",
    )(ids, gram, *parts)


def update_kernel(
    ids_ref, own_ref, other_ref, inverse_ref, back_ref, grad_ref, memory_ref,
    share_ref, out_hbm, out_ref, store_sems,
):
    def columns(step):
        return pl.ds(step * STEP_WIDTH, STEP_WIDTH)

    def store(step):
        cols = columns(step)
        return pltpu.make_async_copy(out_ref.at[:, cols], out_hbm.at[:, cols], store_sems.at[step])

    even = ids_ref[0] == 0
    back = back_ref[:, :192]

    def block(chunk, tile):
        parts = [ref[chunk, row, tile] for ref in (own_ref, other_ref) for row in range(2)]
        return jnp.concatenate(parts, axis=0)

    for step in range(STEPS):
        tiles = [block(step * GROUP + member, tile) for member in range(GROUP) for tile in range(TILES)]
        right = jnp.concatenate(tiles, axis=1)
        one, two, three = (part.astype(BF16) for part in three_parts(right))
        stack = jnp.concatenate([one, one, one, two, two, three], axis=0)
        update = jnp.dot(back, stack, preferred_element_type=F32)
        cols = columns(step)
        merged = grad_ref[:, cols].astype(F32) + memory_ref[:, cols].astype(F32)
        out_ref[:, cols] = (merged - update).astype(BF16)
        store(step).start()

    mine, odd = ids_ref[1], ids_ref[2]

    def natural(tile):
        own0, own1, other0, other1 = (ref[mine, row, tile] for ref in (own_ref, other_ref) for row in range(2))
        return jnp.concatenate(
            [
                jnp.where(even, own0, other0),
                jnp.where(even, other0, own0),
                jnp.where(even, own1, other1),
                jnp.where(even, other1, own1),
            ],
            axis=0,
        )

    right = jnp.concatenate([natural(tile) for tile in range(TILES)], axis=1)
    share = jnp.dot(
        inverse_ref[:, :32], right, precision=lax.Precision.HIGHEST, preferred_element_type=F32
    ) * (1.0 / 8)
    half = WIDTH // 2
    share_ref[...] = jnp.where(odd == 0, share[:, :half], share[:, half:])

    for step in range(STEPS):
        store(step).wait()


def finish(ids, own, other, inverse, back, grad, memory):
    return pl.pallas_call(
        update_kernel,
        out_shape=(
            jax.ShapeDtypeStruct((RANK, WIDTH // 2), F32),
            jax.ShapeDtypeStruct((ROWS, FF), BF16),
        ),
        in_specs=[SMEM] + [VMEM] * 6,
        out_specs=(VMEM, ANY),
        scratch_shapes=[pltpu.VMEM((ROWS, FF), BF16), pltpu.SemaphoreType.DMA((STEPS,))],
        compiler_params=params(16 * MB),
        name="finish",
    )(ids, own, other, inverse, back, grad, memory)


def fetch_kernel(after_ref, grad_hbm, memory_hbm, grad_ref, memory_ref, sems):
    copies = [
        pltpu.make_async_copy(grad_hbm, grad_ref, sems.at[0]),
        pltpu.make_async_copy(memory_hbm, memory_ref, sems.at[1]),
    ]
    for copy in copies:
        copy.start()
    for copy in copies:
        copy.wait()


def fetch(after, grad, memory):
    return pl.pallas_call(
        fetch_kernel,
        out_shape=(pltpu.VMEM((ROWS, FF), BF16), pltpu.VMEM((ROWS, FF), BF16)),
        in_specs=[ANY, ANY, ANY],
        out_specs=(VMEM, VMEM),
        scratch_shapes=[pltpu.SemaphoreType.DMA((2,))],
        compiler_params=params(16 * MB),
        cost_estimate=pl.CostEstimate(flops=10**8, bytes_accessed=14 * 10**6, transcendentals=0),
        name="fetch",
    )(after, grad, memory)


def exchange(value, axes):
    return lax.all_to_all(value, axes, 0, 0, tiled=True)


def swap(value):
    return lax.ppermute(value, "c", [(0, 1), (1, 0)])


def spread(value, axes, count):
    return exchange(jnp.broadcast_to(value[None], (count,) + value.shape), axes)


def resident(value):
    return pltpu.with_memory_space_constraint(value, pltpu.VMEM)


def far(value):
    return pltpu.with_memory_space_constraint(value, pltpu.HBM)


def on_device(gradients, residual, sketch):
    core = lax.axis_index("c")
    block = lax.axis_index(("x", "z4", "z2"))
    ids = jnp.stack([core, block, lax.axis_index("z1")]).astype(jnp.int32)
    far_grad, far_memory = far(gradients[0]), far(residual[0])
    partial, grad, memory = left_sketch(far_grad, far_memory, far(sketch))
    ids, partial = lax.optimization_barrier((ids, partial))
    pair = partial + swap(partial)
    parts = [pair] + [lax.ppermute(pair, "y", [(i, i ^ k) for i in range(4)]) for k in (1, 2, 3)]
    own, other = project(ids, parts, resident(grad), resident(memory))
    terms = own + swap(other)
    terms = exchange(terms.reshape(32, TILES + 1, 8, 128), SPREAD)
    terms = jnp.sum(terms, axis=0)
    terms = jnp.sum(spread(terms, ("z4", "z2"), 4).reshape((4,) + terms.shape), axis=0)
    gathered = spread(terms[:TILES], SPREAD, 32).reshape(CHUNKS, 2, TILES, 8, 128)
    left, inverse, back = factor(ids, terms[TILES], parts)
    gathered, inverse = lax.optimization_barrier((gathered, inverse))
    near_grad, near_memory = fetch(inverse, far_grad, far_memory)
    share, fresh = finish(
        ids, gathered, swap(gathered), inverse, back, resident(near_grad), resident(near_memory)
    )
    return left, share, fresh[None]


def solution(mesh):
    fine = Mesh(mesh.devices.reshape(SIZES), AXES)
    outer, rep = ("y", "c"), ("x", "z4", "z2", "z1")
    return jax.shard_map(
        on_device,
        mesh=fine,
        in_specs=(P(outer, rep, None), P(outer, rep, None), P()),
        out_specs=(P(None, rep), P(None, rep), P(outer, rep, None)),
        check_vma=False,
    )
```

```python
import jax
import jax.numpy as jnp
from jax import lax
from jax.experimental import pallas as pl
from jax.experimental.pallas import tpu as pltpu
from jax.sharding import Mesh
from jax.sharding import PartitionSpec as P

AXES = ("y", "c", "x", "z4", "z2", "z1")
SIZES = (4, 2, 4, 2, 2, 2)
SPREAD = ("y", "x", "z1")
ROWS = 128
FF = 14336
RANK = 32
CHUNKS = 16
WIDTH = FF // CHUNKS
TILES = WIDTH // 128
LOADS = 8
LOAD_WIDTH = FF // LOADS
GROUP = 4
STEPS = CHUNKS // GROUP
STEP_WIDTH = GROUP * WIDTH
F32 = jnp.float32
BF16 = jnp.bfloat16
MB = 1024 * 1024

ANY = pl.BlockSpec(memory_space=pl.ANY)
VMEM = pl.BlockSpec(memory_space=pltpu.VMEM)
SMEM = pl.BlockSpec(memory_space=pltpu.SMEM)


def params(limit):
    return pltpu.CompilerParams(vmem_limit_bytes=limit)


def three_parts(value):
    first = value.astype(BF16).astype(F32)
    rest = value - first
    second = rest.astype(BF16).astype(F32)
    return first, second, rest - second


def sketch_kernel(grad_hbm, memory_hbm, sketch_hbm, out_ref, grad_ref, memory_ref, sketch_ref, sems):
    copies = []
    for step in range(LOADS):
        cols = pl.ds(step * LOAD_WIDTH, LOAD_WIDTH)
        group = [
            pltpu.make_async_copy(src.at[:, cols], dst.at[:, cols], sems.at[step, which])
            for which, (src, dst) in enumerate(
                ((sketch_hbm, sketch_ref), (grad_hbm, grad_ref), (memory_hbm, memory_ref))
            )
        ]
        for copy in group:
            copy.start()
        copies.append(group)
    total = jnp.zeros((RANK, ROWS), F32)
    for step in range(LOADS):
        for copy in copies[step]:
            copy.wait()
        cols = pl.ds(step * LOAD_WIDTH, LOAD_WIDTH)
        probe = sketch_ref[:, cols]
        for block in (grad_ref, memory_ref):
            total += lax.dot_general(
                probe, block[:, cols], (((1,), (1,)), ((), ())), preferred_element_type=F32
            )
    out_ref[...] = total


def left_sketch(grad, memory, sketch):
    return pl.pallas_call(
        sketch_kernel,
        out_shape=(
            jax.ShapeDtypeStruct((RANK, ROWS), F32),
            pltpu.VMEM((ROWS, FF), BF16),
            pltpu.VMEM((ROWS, FF), BF16),
        ),
        in_specs=[ANY, ANY, ANY],
        out_specs=(VMEM, VMEM, VMEM),
        scratch_shapes=[pltpu.VMEM((RANK, FF), BF16), pltpu.SemaphoreType.DMA((LOADS, 3))],
        compiler_params=params(16 * MB),
        name="left_sketch",
    )(grad, memory, sketch)


def mean_of(part_refs):
    one, two, three, four = (ref[...] for ref in part_refs)
    return ((one + two) + (three + four)) * (1.0 / 8)


def project_kernel(ids_ref, *refs):
    part_refs, (grad_ref, memory_ref, own_ref, other_ref) = refs[:4], refs[4:]
    core = ids_ref[0]
    summed = mean_of(part_refs)
    tiled = jnp.concatenate([summed] * 4, axis=0)
    square = lax.dot_general(
        summed, tiled, (((1,), (1,)), ((), ())), precision=lax.Precision.HIGHEST, preferred_element_type=F32
    )
    lane = lax.broadcasted_iota(jnp.int32, (8, 128), 1) // 32
    gram = jnp.zeros((8, 128), F32)
    for group in range(4):
        gram = jnp.where(lane == group, square[8 * group : 8 * group + 8], gram)
    groups = [summed[8 * q : 8 * q + 8] for q in range(4)]
    even = core == 0
    ordered = jnp.concatenate(
        [
            jnp.where(even, groups[0], groups[1]),
            jnp.where(even, groups[2], groups[3]),
            jnp.where(even, groups[1], groups[0]),
            jnp.where(even, groups[3], groups[2]),
        ],
        axis=0,
    )
    left = jnp.concatenate(three_parts(ordered), axis=0).astype(BF16)
    left = jnp.concatenate([left, left], axis=1)

    @pl.loop(0, STEPS, unroll=2)
    def _(step):
        cols = pl.ds(pl.multiple_of(step * STEP_WIDTH, 128), STEP_WIDTH)
        both = jnp.concatenate([grad_ref[:, cols], memory_ref[:, cols]], axis=0)
        product = jnp.dot(left, both, preferred_element_type=F32)
        product = product[:32] + (product[32:64] + product[64:])
        for member in range(GROUP):
            chunk = step * GROUP + member
            for half, ref in enumerate((own_ref, other_ref)):
                for row in range(2):
                    base = 16 * half + 8 * row
                    for tile in range(TILES):
                        left_edge = WIDTH * member + 128 * tile
                        ref[chunk, row, tile] = product[base : base + 8, left_edge : left_edge + 128]
                    ref[chunk, row, TILES] = gram


def project(ids, parts, grad, memory):
    shape = jax.ShapeDtypeStruct((CHUNKS, 2, TILES + 1, 8, 128), F32)
    return pl.pallas_call(
        project_kernel,
        out_shape=(shape, shape),
        in_specs=[SMEM] + [VMEM] * 6,
        out_specs=(VMEM, VMEM),
        compiler_params=params(16 * MB),
        name="project",
    )(ids, *parts, grad, memory)


def factor_kernel(ids_ref, gram_ref, *refs):
    part_refs, (left_ref, inverse_ref, back_ref) = refs[:4], refs[4:]
    core = ids_ref[0]
    rows = lax.broadcasted_iota(jnp.int32, (RANK, 128), 0)
    lanes = lax.broadcasted_iota(jnp.int32, (RANK, 128), 1)
    tile = gram_ref[...] * (1.0 / 8)
    packed = jnp.concatenate([tile] + [pltpu.roll(tile, 128 - 32 * q, 1) for q in (1, 2, 3)], axis=0)
    work = jnp.where(lanes < 32, packed, jnp.where(lanes == rows + 32, 1.0, 0.0))
    basis = mean_of(part_refs)
    scale = jnp.ones((RANK, 128), F32)
    for step in range(RANK):
        column = jnp.broadcast_to(work[:, step : step + 1], (RANK, 128))
        pivot = column[step : step + 1]
        scale = jnp.where(rows == step, pivot, scale)
        factor = jnp.where(rows > step, column / pivot, 0.0)
        work = work - factor * work[step : step + 1]
        basis = basis - factor * basis[step : step + 1]
    scale = lax.rsqrt(scale)
    left = basis * scale
    left_ref[...] = left
    inverse = pltpu.roll(work * scale, 96, 1)
    inverse = jnp.where(lanes < 32, inverse, 0.0)
    inverse_ref[...] = inverse
    solved = lax.dot_general(
        inverse, left, (((0,), (0,)), ((), ())), precision=lax.Precision.HIGHEST, preferred_element_type=F32
    )[:32] * (1.0 / 8)
    even = core == 0
    groups = [solved[8 * q : 8 * q + 8] for q in range(4)]
    ordered = jnp.concatenate(
        [
            jnp.where(even, groups[0], groups[1]),
            jnp.where(even, groups[2], groups[3]),
            jnp.where(even, groups[1], groups[0]),
            jnp.where(even, groups[3], groups[2]),
        ],
        axis=0,
    )
    one, two, three = three_parts(ordered)
    stack = jnp.concatenate([one, two, three, one, two, one, jnp.zeros((64, 128), F32)], axis=0)
    back_ref[...] = stack.T.astype(BF16)


def factor(ids, gram, parts):
    return pl.pallas_call(
        factor_kernel,
        out_shape=(
            jax.ShapeDtypeStruct((RANK, ROWS), F32),
            jax.ShapeDtypeStruct((RANK, 128), F32),
            jax.ShapeDtypeStruct((ROWS, 256), BF16),
        ),
        in_specs=[SMEM] + [VMEM] * 5,
        out_specs=(VMEM, VMEM, VMEM),
        compiler_params=params(16 * MB),
        cost_estimate=pl.CostEstimate(flops=10**9, bytes_accessed=10**7, transcendentals=0),
        name="factor",
    )(ids, gram, *parts)


def update_kernel(
    ids_ref, own_ref, other_ref, inverse_ref, back_ref, grad_ref, memory_ref,
    share_ref, out_hbm, out_ref, store_sems,
):
    def columns(step):
        return pl.ds(step * STEP_WIDTH, STEP_WIDTH)

    def store(step):
        cols = columns(step)
        return pltpu.make_async_copy(out_ref.at[:, cols], out_hbm.at[:, cols], store_sems.at[step])

    even = ids_ref[0] == 0
    back = back_ref[:, :192]

    def block(chunk, tile):
        parts = [ref[chunk, row, tile] for ref in (own_ref, other_ref) for row in range(2)]
        return jnp.concatenate(parts, axis=0)

    for step in range(STEPS):
        tiles = [block(step * GROUP + member, tile) for member in range(GROUP) for tile in range(TILES)]
        right = jnp.concatenate(tiles, axis=1)
        one, two, three = (part.astype(BF16) for part in three_parts(right))
        stack = jnp.concatenate([one, one, one, two, two, three], axis=0)
        update = jnp.dot(back, stack, preferred_element_type=F32)
        cols = columns(step)
        merged = grad_ref[:, cols].astype(F32) + memory_ref[:, cols].astype(F32)
        out_ref[:, cols] = (merged - update).astype(BF16)
        store(step).start()

    mine, odd = ids_ref[1], ids_ref[2]

    def natural(tile):
        own0, own1, other0, other1 = (ref[mine, row, tile] for ref in (own_ref, other_ref) for row in range(2))
        return jnp.concatenate(
            [
                jnp.where(even, own0, other0),
                jnp.where(even, other0, own0),
                jnp.where(even, own1, other1),
                jnp.where(even, other1, own1),
            ],
            axis=0,
        )

    right = jnp.concatenate([natural(tile) for tile in range(TILES)], axis=1)
    share = jnp.dot(
        inverse_ref[:, :32], right, precision=lax.Precision.HIGHEST, preferred_element_type=F32
    ) * (1.0 / 8)
    half = WIDTH // 2
    share_ref[...] = jnp.where(odd == 0, share[:, :half], share[:, half:])

    for step in range(STEPS):
        store(step).wait()


def finish(ids, own, other, inverse, back, grad, memory):
    return pl.pallas_call(
        update_kernel,
        out_shape=(
            jax.ShapeDtypeStruct((RANK, WIDTH // 2), F32),
            jax.ShapeDtypeStruct((ROWS, FF), BF16),
        ),
        in_specs=[SMEM] + [VMEM] * 6,
        out_specs=(VMEM, ANY),
        scratch_shapes=[pltpu.VMEM((ROWS, FF), BF16), pltpu.SemaphoreType.DMA((STEPS,))],
        compiler_params=params(16 * MB),
        name="finish",
    )(ids, own, other, inverse, back, grad, memory)


def fetch_kernel(after_ref, grad_hbm, memory_hbm, grad_ref, memory_ref, sems):
    copies = [
        pltpu.make_async_copy(grad_hbm, grad_ref, sems.at[0]),
        pltpu.make_async_copy(memory_hbm, memory_ref, sems.at[1]),
    ]
    for copy in copies:
        copy.start()
    for copy in copies:
        copy.wait()


def fetch(after, grad, memory):
    return pl.pallas_call(
        fetch_kernel,
        out_shape=(pltpu.VMEM((ROWS, FF), BF16), pltpu.VMEM((ROWS, FF), BF16)),
        in_specs=[ANY, ANY, ANY],
        out_specs=(VMEM, VMEM),
        scratch_shapes=[pltpu.SemaphoreType.DMA((2,))],
        compiler_params=params(16 * MB),
        cost_estimate=pl.CostEstimate(flops=10**8, bytes_accessed=14 * 10**6, transcendentals=0),
        name="fetch",
    )(after, grad, memory)


def exchange(value, axes):
    return lax.all_to_all(value, axes, 0, 0, tiled=True)


def swap(value):
    return lax.ppermute(value, "c", [(0, 1), (1, 0)])


def four(value, axes):
    one, three, two = (lax.ppermute(value, axes, [(i, i ^ k) for i in range(4)]) for k in (1, 3, 2))
    return value, one, two, three


def spread(value, axes, count):
    return exchange(jnp.broadcast_to(value[None], (count,) + value.shape), axes)


def resident(value):
    return pltpu.with_memory_space_constraint(value, pltpu.VMEM)


def far(value):
    return pltpu.with_memory_space_constraint(value, pltpu.HBM)


def on_device(gradients, residual, sketch):
    core = lax.axis_index("c")
    block = lax.axis_index(("x", "z4", "z2"))
    ids = jnp.stack([core, block, lax.axis_index("z1")]).astype(jnp.int32)
    far_grad, far_memory = far(gradients[0]), far(residual[0])
    partial, grad, memory = left_sketch(far_grad, far_memory, far(sketch))
    ids, partial = lax.optimization_barrier((ids, partial))
    pair = partial + swap(partial)
    parts = four(pair, "y")
    own, other = project(ids, parts, resident(grad), resident(memory))
    terms = own + swap(other)
    terms = exchange(terms.reshape(32, TILES + 1, 8, 128), SPREAD)
    terms = jnp.sum(terms, axis=0)
    one, two, three, last = four(terms, ("z4", "z2"))
    terms = (one + two) + (three + last)
    gathered = spread(terms[:TILES], SPREAD, 32).reshape(CHUNKS, 2, TILES, 8, 128)
    left, inverse, back = factor(ids, terms[TILES], parts)
    gathered, inverse = lax.optimization_barrier((gathered, inverse))
    near_grad, near_memory = fetch(inverse, far_grad, far_memory)
    share, fresh = finish(
        ids, gathered, swap(gathered), inverse, back, resident(near_grad), resident(near_memory)
    )
    return left, share, fresh[None]


def solution(mesh):
    fine = Mesh(mesh.devices.reshape(SIZES), AXES)
    outer, rep = ("y", "c"), ("x", "z4", "z2", "z1")
    return jax.shard_map(
        on_device,
        mesh=fine,
        in_specs=(P(outer, rep, None), P(outer, rep, None), P()),
        out_specs=(P(None, rep), P(None, rep), P(outer, rep, None)),
        check_vma=False,
    )
```

```python
import jax
import jax.numpy as jnp
from jax import lax
from jax.experimental import pallas as pl
from jax.experimental.pallas import tpu as pltpu
from jax.sharding import Mesh
from jax.sharding import PartitionSpec as P

AXES = ("y", "c", "x", "z4", "z2", "z1")
SIZES = (4, 2, 4, 2, 2, 2)
SPREAD = ("y", "x", "z1")
ROWS = 128
FF = 14336
RANK = 32
CHUNKS = 16
WIDTH = FF // CHUNKS
TILES = WIDTH // 128
LOADS = 8
LOAD_WIDTH = FF // LOADS
GROUP = 4
STEPS = CHUNKS // GROUP
STEP_WIDTH = GROUP * WIDTH
F32 = jnp.float32
BF16 = jnp.bfloat16
MB = 1024 * 1024

ANY = pl.BlockSpec(memory_space=pl.ANY)
VMEM = pl.BlockSpec(memory_space=pltpu.VMEM)
SMEM = pl.BlockSpec(memory_space=pltpu.SMEM)


def params(limit):
    return pltpu.CompilerParams(vmem_limit_bytes=limit)


def three_parts(value):
    first = value.astype(BF16).astype(F32)
    rest = value - first
    second = rest.astype(BF16).astype(F32)
    return first, second, rest - second


def sketch_kernel(grad_hbm, memory_hbm, sketch_hbm, out_ref, grad_ref, memory_ref, sketch_ref, sems):
    copies = []
    for step in range(LOADS):
        cols = pl.ds(step * LOAD_WIDTH, LOAD_WIDTH)
        group = [
            pltpu.make_async_copy(src.at[:, cols], dst.at[:, cols], sems.at[step, which])
            for which, (src, dst) in enumerate(
                ((sketch_hbm, sketch_ref), (grad_hbm, grad_ref), (memory_hbm, memory_ref))
            )
        ]
        for copy in group:
            copy.start()
        copies.append(group)
    total = jnp.zeros((RANK, ROWS), F32)
    for step in range(LOADS):
        for copy in copies[step]:
            copy.wait()
        cols = pl.ds(step * LOAD_WIDTH, LOAD_WIDTH)
        probe = sketch_ref[:, cols]
        for block in (grad_ref, memory_ref):
            total += lax.dot_general(
                probe, block[:, cols], (((1,), (1,)), ((), ())), preferred_element_type=F32
            )
    out_ref[...] = total


def left_sketch(grad, memory, sketch):
    return pl.pallas_call(
        sketch_kernel,
        out_shape=(
            jax.ShapeDtypeStruct((RANK, ROWS), F32),
            pltpu.VMEM((ROWS, FF), BF16),
            pltpu.VMEM((ROWS, FF), BF16),
        ),
        in_specs=[ANY, ANY, ANY],
        out_specs=(VMEM, VMEM, VMEM),
        scratch_shapes=[pltpu.VMEM((RANK, FF), BF16), pltpu.SemaphoreType.DMA((LOADS, 3))],
        compiler_params=params(16 * MB),
        name="left_sketch",
    )(grad, memory, sketch)


def mean_of(part_refs):
    one, two, three, four = (ref[...] for ref in part_refs)
    return ((one + two) + (three + four)) * (1.0 / 8)


def project_kernel(ids_ref, *refs):
    part_refs, (grad_ref, memory_ref, own_ref, other_ref) = refs[:4], refs[4:]
    core = ids_ref[0]
    summed = mean_of(part_refs)
    tiled = jnp.concatenate([summed] * 4, axis=0)
    square = lax.dot_general(
        summed, tiled, (((1,), (1,)), ((), ())), precision=lax.Precision.HIGHEST, preferred_element_type=F32
    )
    lane = lax.broadcasted_iota(jnp.int32, (8, 128), 1) // 32
    gram = jnp.zeros((8, 128), F32)
    for group in range(4):
        gram = jnp.where(lane == group, square[8 * group : 8 * group + 8], gram)
    groups = [summed[8 * q : 8 * q + 8] for q in range(4)]
    even = core == 0
    ordered = jnp.concatenate(
        [
            jnp.where(even, groups[0], groups[1]),
            jnp.where(even, groups[2], groups[3]),
            jnp.where(even, groups[1], groups[0]),
            jnp.where(even, groups[3], groups[2]),
        ],
        axis=0,
    )
    left = jnp.concatenate(three_parts(ordered), axis=0).astype(BF16)
    left = jnp.concatenate([left, left], axis=1)

    @pl.loop(0, STEPS, unroll=2)
    def _(step):
        cols = pl.ds(pl.multiple_of(step * STEP_WIDTH, 128), STEP_WIDTH)
        both = jnp.concatenate([grad_ref[:, cols], memory_ref[:, cols]], axis=0)
        product = jnp.dot(left, both, preferred_element_type=F32)
        product = product[:32] + (product[32:64] + product[64:])
        for member in range(GROUP):
            chunk = step * GROUP + member
            for half, ref in enumerate((own_ref, other_ref)):
                for row in range(2):
                    base = 16 * half + 8 * row
                    for tile in range(TILES):
                        left_edge = WIDTH * member + 128 * tile
                        ref[chunk, row, tile] = product[base : base + 8, left_edge : left_edge + 128]
                    ref[chunk, row, TILES] = gram


def project(ids, parts, grad, memory):
    shape = jax.ShapeDtypeStruct((CHUNKS, 2, TILES + 1, 8, 128), F32)
    return pl.pallas_call(
        project_kernel,
        out_shape=(shape, shape),
        in_specs=[SMEM] + [VMEM] * 6,
        out_specs=(VMEM, VMEM),
        compiler_params=params(16 * MB),
        name="project",
    )(ids, *parts, grad, memory)


def factor_kernel(ids_ref, gram_ref, *refs):
    part_refs, (left_ref, inverse_ref, back_ref) = refs[:4], refs[4:]
    core = ids_ref[0]
    row = lax.broadcasted_iota(jnp.int32, (8, 128), 0)
    lane = lax.broadcasted_iota(jnp.int32, (8, 128), 1)
    tile = gram_ref[...] * (1.0 / 8)
    work, scales = [], []
    for q in range(4):
        part = pltpu.roll(tile, 128 - 32 * q, 1) if q else tile
        work.append(jnp.where(lane < 32, part, jnp.where(lane == row + (32 + 8 * q), 1.0, 0.0)))
    summed = mean_of(part_refs)
    basis = [summed[8 * q : 8 * q + 8] for q in range(4)]
    for p in range(4):
        below = range(p, 4)
        columns = [
            {g: jnp.broadcast_to(work[g][:, 8 * p + q : 8 * p + q + 1], (8, 128)) for g in below} for q in range(8)
        ]
        scale = jnp.ones((8, 128), F32)
        for q in range(8):
            pivot = columns[q][p][q : q + 1]
            scale = jnp.where(row == q, pivot, scale)
            ratio = 1.0 / pivot
            factors = {g: columns[q][g] * ratio for g in below}
            factors[p] = jnp.where(row > q, factors[p], 0.0)
            for later in range(q + 1, 8):
                edge = columns[later][p][q : q + 1]
                for g in below:
                    columns[later][g] = columns[later][g] - factors[g] * edge
            work_row, basis_row = work[p][q : q + 1], basis[p][q : q + 1]
            for g in below:
                work[g] = work[g] - factors[g] * work_row
                basis[g] = basis[g] - factors[g] * basis_row
        scales.append(lax.rsqrt(scale))
    scale = jnp.concatenate(scales, axis=0)
    work, basis = jnp.concatenate(work, axis=0), jnp.concatenate(basis, axis=0)
    lanes = lax.broadcasted_iota(jnp.int32, (RANK, 128), 1)
    left = basis * scale
    left_ref[...] = left
    inverse = pltpu.roll(work * scale, 96, 1)
    inverse = jnp.where(lanes < 32, inverse, 0.0)
    inverse_ref[...] = inverse
    solved = lax.dot_general(
        inverse, left, (((0,), (0,)), ((), ())), precision=lax.Precision.HIGHEST, preferred_element_type=F32
    )[:32] * (1.0 / 8)
    even = core == 0
    groups = [solved[8 * q : 8 * q + 8] for q in range(4)]
    ordered = jnp.concatenate(
        [
            jnp.where(even, groups[0], groups[1]),
            jnp.where(even, groups[2], groups[3]),
            jnp.where(even, groups[1], groups[0]),
            jnp.where(even, groups[3], groups[2]),
        ],
        axis=0,
    )
    one, two, three = three_parts(ordered)
    stack = jnp.concatenate([one, two, three, one, two, one, jnp.zeros((64, 128), F32)], axis=0)
    back_ref[...] = stack.T.astype(BF16)


def factor(ids, gram, parts):
    return pl.pallas_call(
        factor_kernel,
        out_shape=(
            jax.ShapeDtypeStruct((RANK, ROWS), F32),
            jax.ShapeDtypeStruct((RANK, 128), F32),
            jax.ShapeDtypeStruct((ROWS, 256), BF16),
        ),
        in_specs=[SMEM] + [VMEM] * 5,
        out_specs=(VMEM, VMEM, VMEM),
        compiler_params=params(16 * MB),
        cost_estimate=pl.CostEstimate(flops=2 * 10**10, bytes_accessed=10**7, transcendentals=0),
        name="factor",
    )(ids, gram, *parts)


def update_kernel(
    ids_ref, own_ref, other_ref, inverse_ref, back_ref, grad_ref, memory_ref,
    share_ref, out_hbm, out_ref, store_sems,
):
    def columns(step):
        return pl.ds(step * STEP_WIDTH, STEP_WIDTH)

    def store(step):
        cols = columns(step)
        return pltpu.make_async_copy(out_ref.at[:, cols], out_hbm.at[:, cols], store_sems.at[step])

    even = ids_ref[0] == 0
    back = back_ref[:, :192]

    def block(chunk, tile):
        parts = [ref[chunk, row, tile] for ref in (own_ref, other_ref) for row in range(2)]
        return jnp.concatenate(parts, axis=0)

    for step in range(STEPS):
        tiles = [block(step * GROUP + member, tile) for member in range(GROUP) for tile in range(TILES)]
        right = jnp.concatenate(tiles, axis=1)
        one, two, three = (part.astype(BF16) for part in three_parts(right))
        stack = jnp.concatenate([one, one, one, two, two, three], axis=0)
        update = jnp.dot(back, stack, preferred_element_type=F32)
        cols = columns(step)
        merged = grad_ref[:, cols].astype(F32) + memory_ref[:, cols].astype(F32)
        out_ref[:, cols] = (merged - update).astype(BF16)
        store(step).start()

    mine, odd = ids_ref[1], ids_ref[2]

    def natural(tile):
        own0, own1, other0, other1 = (ref[mine, row, tile] for ref in (own_ref, other_ref) for row in range(2))
        return jnp.concatenate(
            [
                jnp.where(even, own0, other0),
                jnp.where(even, other0, own0),
                jnp.where(even, own1, other1),
                jnp.where(even, other1, own1),
            ],
            axis=0,
        )

    right = jnp.concatenate([natural(tile) for tile in range(TILES)], axis=1)
    share = jnp.dot(
        inverse_ref[:, :32], right, precision=lax.Precision.HIGHEST, preferred_element_type=F32
    ) * (1.0 / 8)
    half = WIDTH // 2
    share_ref[...] = jnp.where(odd == 0, share[:, :half], share[:, half:])

    for step in range(STEPS):
        store(step).wait()


def finish(ids, own, other, inverse, back, grad, memory):
    return pl.pallas_call(
        update_kernel,
        out_shape=(
            jax.ShapeDtypeStruct((RANK, WIDTH // 2), F32),
            jax.ShapeDtypeStruct((ROWS, FF), BF16),
        ),
        in_specs=[SMEM] + [VMEM] * 6,
        out_specs=(VMEM, ANY),
        scratch_shapes=[pltpu.VMEM((ROWS, FF), BF16), pltpu.SemaphoreType.DMA((STEPS,))],
        compiler_params=params(16 * MB),
        name="finish",
    )(ids, own, other, inverse, back, grad, memory)


def exchange(value, axes):
    return lax.all_to_all(value, axes, 0, 0, tiled=True)


def swap(value):
    return lax.ppermute(value, "c", [(0, 1), (1, 0)])


def four(value, axes):
    one, three, two = (lax.ppermute(value, axes, [(i, i ^ k) for i in range(4)]) for k in (1, 3, 2))
    return value, one, two, three


def spread(value, axes, count):
    return exchange(jnp.broadcast_to(value[None], (count,) + value.shape), axes)


def resident(value):
    return pltpu.with_memory_space_constraint(value, pltpu.VMEM)


def far(value):
    return pltpu.with_memory_space_constraint(value, pltpu.HBM)


def on_device(gradients, residual, sketch):
    core = lax.axis_index("c")
    block = lax.axis_index(("x", "z4", "z2"))
    ids = jnp.stack([core, block, lax.axis_index("z1")]).astype(jnp.int32)
    far_grad, far_memory = far(gradients[0]), far(residual[0])
    partial, grad, memory = left_sketch(far_grad, far_memory, far(sketch))
    ids, partial = lax.optimization_barrier((ids, partial))
    pair = partial + swap(partial)
    parts = four(pair, "y")
    own, other = project(ids, parts, resident(grad), resident(memory))
    terms = own + swap(other)
    terms = exchange(terms.reshape(32, TILES + 1, 8, 128), SPREAD)
    terms = jnp.sum(terms, axis=0)
    one, two, three, last = four(terms, ("z4", "z2"))
    terms = (one + two) + (three + last)
    gathered = spread(terms[:TILES], SPREAD, 32).reshape(CHUNKS, 2, TILES, 8, 128)
    gathered, gram = lax.optimization_barrier((gathered, terms[TILES]))
    left, inverse, back = factor(ids, gram, parts)
    share, fresh = finish(
        ids, gathered, swap(gathered), inverse, back, resident(gradients[0]), resident(residual[0])
    )
    return left, share, fresh[None]


def solution(mesh):
    fine = Mesh(mesh.devices.reshape(SIZES), AXES)
    outer, rep = ("y", "c"), ("x", "z4", "z2", "z1")
    return jax.shard_map(
        on_device,
        mesh=fine,
        in_specs=(P(outer, rep, None), P(outer, rep, None), P()),
        out_specs=(P(None, rep), P(None, rep), P(outer, rep, None)),
        check_vma=False,
    )
```

```python
import jax
import jax.numpy as jnp
from jax import lax
from jax.experimental import pallas as pl
from jax.experimental.pallas import tpu as pltpu
from jax.sharding import Mesh
from jax.sharding import PartitionSpec as P

AXES = ("y", "c", "x", "z4", "z2", "z1")
SIZES = (4, 2, 4, 2, 2, 2)
SPREAD = ("y", "x", "z1")
ROWS = 128
FF = 14336
RANK = 32
CHUNKS = 16
WIDTH = FF // CHUNKS
TILES = WIDTH // 128
LOADS = 8
LOAD_WIDTH = FF // LOADS
GROUP = 4
STEPS = CHUNKS // GROUP
STEP_WIDTH = GROUP * WIDTH
F32 = jnp.float32
BF16 = jnp.bfloat16
MB = 1024 * 1024

ANY = pl.BlockSpec(memory_space=pl.ANY)
VMEM = pl.BlockSpec(memory_space=pltpu.VMEM)
SMEM = pl.BlockSpec(memory_space=pltpu.SMEM)


def params(limit):
    return pltpu.CompilerParams(vmem_limit_bytes=limit)


def three_parts(value):
    first = value.astype(BF16).astype(F32)
    rest = value - first
    second = rest.astype(BF16).astype(F32)
    return first, second, rest - second


def product(sketch, block):
    return lax.dot_general(sketch, block, (((1,), (1,)), ((), ())), preferred_element_type=F32)


def first_kernel(grad_hbm, sketch_hbm, out_ref, grad_ref, sketch_ref, sems):
    copies = []
    for step in range(LOADS):
        cols = pl.ds(step * LOAD_WIDTH, LOAD_WIDTH)
        group = [
            pltpu.make_async_copy(src.at[:, cols], dst.at[:, cols], sems.at[step, which])
            for which, (src, dst) in enumerate(((sketch_hbm, sketch_ref), (grad_hbm, grad_ref)))
        ]
        for copy in group:
            copy.start()
        copies.append(group)
    total = jnp.zeros((RANK, ROWS), F32)
    for step in range(LOADS):
        for copy in copies[step]:
            copy.wait()
        cols = pl.ds(step * LOAD_WIDTH, LOAD_WIDTH)
        total += product(sketch_ref[:, cols], grad_ref[:, cols])
    out_ref[...] = total


def second_kernel(first_ref, sketch_ref, memory_ref, out_ref):
    out_ref[...] = first_ref[...] + product(sketch_ref[...], memory_ref[...])


def left_sketch(grad, memory, sketch):
    first, near_grad, near_sketch = pl.pallas_call(
        first_kernel,
        out_shape=(
            jax.ShapeDtypeStruct((RANK, ROWS), F32),
            pltpu.VMEM((ROWS, FF), BF16),
            pltpu.VMEM((RANK, FF), BF16),
        ),
        in_specs=[ANY, ANY],
        out_specs=(VMEM,) * 3,
        scratch_shapes=[pltpu.SemaphoreType.DMA((LOADS, 2))],
        compiler_params=params(16 * MB),
        cost_estimate=pl.CostEstimate(flops=2 * 10**10, bytes_accessed=10**7, transcendentals=0),
        name="left_first",
    )(grad, sketch)
    total = pl.pallas_call(
        second_kernel,
        out_shape=jax.ShapeDtypeStruct((RANK, ROWS), F32),
        in_specs=[VMEM] * 3,
        out_specs=VMEM,
        compiler_params=params(16 * MB),
        name="left_second",
    )(first, resident(near_sketch), resident(memory))
    return total, near_grad


def mean_of(part_refs):
    one, two, three, four = (ref[...] for ref in part_refs)
    return ((one + two) + (three + four)) * (1.0 / 8)


def project_kernel(ids_ref, *refs):
    part_refs, (grad_ref, memory_ref, own_ref, other_ref) = refs[:4], refs[4:]
    core = ids_ref[0]
    summed = mean_of(part_refs)
    tiled = jnp.concatenate([summed] * 4, axis=0)
    square = lax.dot_general(
        summed, tiled, (((1,), (1,)), ((), ())), precision=lax.Precision.HIGHEST, preferred_element_type=F32
    )
    lane = lax.broadcasted_iota(jnp.int32, (8, 128), 1) // 32
    gram = jnp.zeros((8, 128), F32)
    for group in range(4):
        gram = jnp.where(lane == group, square[8 * group : 8 * group + 8], gram)
    groups = [summed[8 * q : 8 * q + 8] for q in range(4)]
    even = core == 0
    ordered = jnp.concatenate(
        [
            jnp.where(even, groups[0], groups[1]),
            jnp.where(even, groups[2], groups[3]),
            jnp.where(even, groups[1], groups[0]),
            jnp.where(even, groups[3], groups[2]),
        ],
        axis=0,
    )
    left = jnp.concatenate(three_parts(ordered), axis=0).astype(BF16)
    left = jnp.concatenate([left, left], axis=1)

    @pl.loop(0, STEPS, unroll=2)
    def _(step):
        cols = pl.ds(pl.multiple_of(step * STEP_WIDTH, 128), STEP_WIDTH)
        both = jnp.concatenate([grad_ref[:, cols], memory_ref[:, cols]], axis=0)
        product = jnp.dot(left, both, preferred_element_type=F32)
        product = product[:32] + (product[32:64] + product[64:])
        for member in range(GROUP):
            chunk = step * GROUP + member
            for half, ref in enumerate((own_ref, other_ref)):
                for row in range(2):
                    base = 16 * half + 8 * row
                    for tile in range(TILES):
                        left_edge = WIDTH * member + 128 * tile
                        ref[chunk, row, tile] = product[base : base + 8, left_edge : left_edge + 128]
                    ref[chunk, row, TILES] = gram


def project(ids, parts, grad, memory):
    shape = jax.ShapeDtypeStruct((CHUNKS, 2, TILES + 1, 8, 128), F32)
    return pl.pallas_call(
        project_kernel,
        out_shape=(shape, shape),
        in_specs=[SMEM] + [VMEM] * 6,
        out_specs=(VMEM, VMEM),
        compiler_params=params(16 * MB),
        name="project",
    )(ids, *parts, grad, memory)


def factor_kernel(ids_ref, gram_ref, *refs):
    part_refs, (left_ref, inverse_ref, back_ref) = refs[:4], refs[4:]
    core = ids_ref[0]
    row = lax.broadcasted_iota(jnp.int32, (8, 128), 0)
    lane = lax.broadcasted_iota(jnp.int32, (8, 128), 1)
    tile = gram_ref[...] * (1.0 / 8)
    work, scales = [], []
    for q in range(4):
        part = pltpu.roll(tile, 128 - 32 * q, 1) if q else tile
        work.append(jnp.where(lane < 32, part, jnp.where(lane == row + (32 + 8 * q), 1.0, 0.0)))
    summed = mean_of(part_refs)
    basis = [summed[8 * q : 8 * q + 8] for q in range(4)]
    for p in range(4):
        below = range(p, 4)
        columns = [
            {g: jnp.broadcast_to(work[g][:, 8 * p + q : 8 * p + q + 1], (8, 128)) for g in below} for q in range(8)
        ]
        scale = jnp.ones((8, 128), F32)
        for q in range(8):
            pivot = columns[q][p][q : q + 1]
            scale = jnp.where(row == q, pivot, scale)
            ratio = 1.0 / pivot
            factors = {g: columns[q][g] * ratio for g in below}
            factors[p] = jnp.where(row > q, factors[p], 0.0)
            for later in range(q + 1, 8):
                edge = columns[later][p][q : q + 1]
                for g in below:
                    columns[later][g] = columns[later][g] - factors[g] * edge
            work_row, basis_row = work[p][q : q + 1], basis[p][q : q + 1]
            for g in below:
                work[g] = work[g] - factors[g] * work_row
                basis[g] = basis[g] - factors[g] * basis_row
        scales.append(lax.rsqrt(scale))
    scale = jnp.concatenate(scales, axis=0)
    work, basis = jnp.concatenate(work, axis=0), jnp.concatenate(basis, axis=0)
    lanes = lax.broadcasted_iota(jnp.int32, (RANK, 128), 1)
    left = basis * scale
    left_ref[...] = left
    inverse = pltpu.roll(work * scale, 96, 1)
    inverse = jnp.where(lanes < 32, inverse, 0.0)
    inverse_ref[...] = inverse
    solved = lax.dot_general(
        inverse, left, (((0,), (0,)), ((), ())), precision=lax.Precision.HIGHEST, preferred_element_type=F32
    )[:32] * (1.0 / 8)
    even = core == 0
    groups = [solved[8 * q : 8 * q + 8] for q in range(4)]
    ordered = jnp.concatenate(
        [
            jnp.where(even, groups[0], groups[1]),
            jnp.where(even, groups[2], groups[3]),
            jnp.where(even, groups[1], groups[0]),
            jnp.where(even, groups[3], groups[2]),
        ],
        axis=0,
    )
    one, two, three = three_parts(ordered)
    stack = jnp.concatenate([one, two, three, one, two, one, jnp.zeros((64, 128), F32)], axis=0)
    back_ref[...] = stack.T.astype(BF16)


def factor(ids, gram, parts):
    return pl.pallas_call(
        factor_kernel,
        out_shape=(
            jax.ShapeDtypeStruct((RANK, ROWS), F32),
            jax.ShapeDtypeStruct((RANK, 128), F32),
            jax.ShapeDtypeStruct((ROWS, 256), BF16),
        ),
        in_specs=[SMEM] + [VMEM] * 5,
        out_specs=(VMEM, VMEM, VMEM),
        compiler_params=params(16 * MB),
        cost_estimate=pl.CostEstimate(flops=2 * 10**10, bytes_accessed=10**7, transcendentals=0),
        name="factor",
    )(ids, gram, *parts)


def update_kernel(
    ids_ref, own_ref, other_ref, inverse_ref, back_ref, grad_ref, memory_ref,
    share_ref, out_hbm, out_ref, store_sems,
):
    def columns(step):
        return pl.ds(step * STEP_WIDTH, STEP_WIDTH)

    def store(step):
        cols = columns(step)
        return pltpu.make_async_copy(out_ref.at[:, cols], out_hbm.at[:, cols], store_sems.at[step])

    even = ids_ref[0] == 0
    back = back_ref[:, :192]

    def block(chunk, tile):
        parts = [ref[chunk, row, tile] for ref in (own_ref, other_ref) for row in range(2)]
        return jnp.concatenate(parts, axis=0)

    for step in range(STEPS):
        tiles = [block(step * GROUP + member, tile) for member in range(GROUP) for tile in range(TILES)]
        right = jnp.concatenate(tiles, axis=1)
        one, two, three = (part.astype(BF16) for part in three_parts(right))
        stack = jnp.concatenate([one, one, one, two, two, three], axis=0)
        update = jnp.dot(back, stack, preferred_element_type=F32)
        cols = columns(step)
        merged = grad_ref[:, cols].astype(F32) + memory_ref[:, cols].astype(F32)
        out_ref[:, cols] = (merged - update).astype(BF16)
        store(step).start()

    mine, odd = ids_ref[1], ids_ref[2]

    def natural(tile):
        own0, own1, other0, other1 = (ref[mine, row, tile] for ref in (own_ref, other_ref) for row in range(2))
        return jnp.concatenate(
            [
                jnp.where(even, own0, other0),
                jnp.where(even, other0, own0),
                jnp.where(even, own1, other1),
                jnp.where(even, other1, own1),
            ],
            axis=0,
        )

    right = jnp.concatenate([natural(tile) for tile in range(TILES)], axis=1)
    share = jnp.dot(
        inverse_ref[:, :32], right, precision=lax.Precision.HIGHEST, preferred_element_type=F32
    ) * (1.0 / 8)
    half = WIDTH // 2
    share_ref[...] = jnp.where(odd == 0, share[:, :half], share[:, half:])

    for step in range(STEPS):
        store(step).wait()


def finish(ids, own, other, inverse, back, grad, memory):
    return pl.pallas_call(
        update_kernel,
        out_shape=(
            jax.ShapeDtypeStruct((RANK, WIDTH // 2), F32),
            jax.ShapeDtypeStruct((ROWS, FF), BF16),
        ),
        in_specs=[SMEM] + [VMEM] * 6,
        out_specs=(VMEM, ANY),
        scratch_shapes=[pltpu.VMEM((ROWS, FF), BF16), pltpu.SemaphoreType.DMA((STEPS,))],
        compiler_params=params(16 * MB),
        name="finish",
    )(ids, own, other, inverse, back, grad, memory)


def exchange(value, axes):
    return lax.all_to_all(value, axes, 0, 0, tiled=True)


def swap(value):
    return lax.ppermute(value, "c", [(0, 1), (1, 0)])


def four(value, axes):
    three, two, one = (lax.ppermute(value, axes, [(i, i ^ k) for i in range(4)]) for k in (3, 2, 1))
    return value, one, two, three


def spread(value, axes, count):
    return exchange(jnp.broadcast_to(value[None], (count,) + value.shape), axes)


def resident(value):
    return pltpu.with_memory_space_constraint(value, pltpu.VMEM)


def far(value):
    return pltpu.with_memory_space_constraint(value, pltpu.HBM)


def on_device(gradients, residual, sketch):
    core = lax.axis_index("c")
    block = lax.axis_index(("x", "z4", "z2"))
    ids = jnp.stack([core, block, lax.axis_index("z1")]).astype(jnp.int32)
    far_grad = far(gradients[0])
    partial, grad = left_sketch(far_grad, residual[0], far(sketch))
    ids, partial = lax.optimization_barrier((ids, partial))
    pair = partial + swap(partial)
    parts = four(pair, "y")
    own, other = project(ids, parts, resident(grad), resident(residual[0]))
    terms = own + swap(other)
    terms = exchange(terms.reshape(32, TILES + 1, 8, 128), SPREAD)
    terms = jnp.sum(terms, axis=0)
    one, two, three, last = four(terms, ("z4", "z2"))
    terms = (one + two) + (three + last)
    gathered = spread(terms[:TILES], SPREAD, 32).reshape(CHUNKS, 2, TILES, 8, 128)
    gathered, gram = lax.optimization_barrier((gathered, terms[TILES]))
    left, inverse, back = factor(ids, gram, parts)
    share, fresh = finish(
        ids, gathered, swap(gathered), inverse, back, resident(gradients[0]), resident(residual[0])
    )
    return left, share, fresh[None]


def solution(mesh):
    fine = Mesh(mesh.devices.reshape(SIZES), AXES)
    outer, rep = ("y", "c"), ("x", "z4", "z2", "z1")
    return jax.shard_map(
        on_device,
        mesh=fine,
        in_specs=(P(outer, rep, None), P(outer, rep, None), P()),
        out_specs=(P(None, rep), P(None, rep), P(outer, rep, None)),
        check_vma=False,
    )
```

```python
import jax
import jax.numpy as jnp
from jax import lax
from jax.experimental import pallas as pl
from jax.experimental.pallas import tpu as pltpu
from jax.sharding import Mesh
from jax.sharding import PartitionSpec as P

AXES = ("y", "c", "x", "z4", "z2", "z1")
SIZES = (4, 2, 4, 2, 2, 2)
SPREAD = ("y", "x", "z1")
ROWS = 128
FF = 14336
RANK = 32
CHUNKS = 16
WIDTH = FF // CHUNKS
TILES = WIDTH // 128
LOADS = 8
LOAD_WIDTH = FF // LOADS
GROUP = 4
STEPS = CHUNKS // GROUP
STEP_WIDTH = GROUP * WIDTH
LAST_GROUP = 2
LAST_STEPS = CHUNKS // LAST_GROUP
LAST_WIDTH = LAST_GROUP * WIDTH
F32 = jnp.float32
BF16 = jnp.bfloat16
MB = 1024 * 1024

ANY = pl.BlockSpec(memory_space=pl.ANY)
VMEM = pl.BlockSpec(memory_space=pltpu.VMEM)
SMEM = pl.BlockSpec(memory_space=pltpu.SMEM)


def params(limit):
    return pltpu.CompilerParams(vmem_limit_bytes=limit)


def three_parts(value):
    first = value.astype(BF16).astype(F32)
    rest = value - first
    second = rest.astype(BF16).astype(F32)
    return first, second, rest - second


def product(sketch, block):
    return lax.dot_general(sketch, block, (((1,), (1,)), ((), ())), preferred_element_type=F32)


def first_kernel(grad_hbm, sketch_hbm, out_ref, grad_ref, sketch_ref, sems):
    copies = []
    for step in range(LOADS):
        cols = pl.ds(step * LOAD_WIDTH, LOAD_WIDTH)
        group = [
            pltpu.make_async_copy(src.at[:, cols], dst.at[:, cols], sems.at[step, which])
            for which, (src, dst) in enumerate(((sketch_hbm, sketch_ref), (grad_hbm, grad_ref)))
        ]
        for copy in group:
            copy.start()
        copies.append(group)
    total = jnp.zeros((RANK, ROWS), F32)
    for step in range(LOADS):
        for copy in copies[step]:
            copy.wait()
        cols = pl.ds(step * LOAD_WIDTH, LOAD_WIDTH)
        total += product(sketch_ref[:, cols], grad_ref[:, cols])
    out_ref[...] = total


def second_kernel(first_ref, sketch_ref, memory_ref, out_ref):
    out_ref[...] = first_ref[...] + product(sketch_ref[...], memory_ref[...])


def left_sketch(grad, memory, sketch):
    first, near_grad, near_sketch = pl.pallas_call(
        first_kernel,
        out_shape=(
            jax.ShapeDtypeStruct((RANK, ROWS), F32),
            pltpu.VMEM((ROWS, FF), BF16),
            pltpu.VMEM((RANK, FF), BF16),
        ),
        in_specs=[ANY, ANY],
        out_specs=(VMEM,) * 3,
        scratch_shapes=[pltpu.SemaphoreType.DMA((LOADS, 2))],
        compiler_params=params(16 * MB),
        cost_estimate=pl.CostEstimate(flops=2 * 10**10, bytes_accessed=10**7, transcendentals=0),
        name="left_first",
    )(grad, sketch)
    total = pl.pallas_call(
        second_kernel,
        out_shape=jax.ShapeDtypeStruct((RANK, ROWS), F32),
        in_specs=[VMEM] * 3,
        out_specs=VMEM,
        compiler_params=params(16 * MB),
        name="left_second",
    )(first, resident(near_sketch), resident(memory))
    return total, near_grad


def mean_of(part_refs):
    one, two, three, four = (ref[...] for ref in part_refs)
    return ((one + two) + (three + four)) * (1.0 / 8)


def project_kernel(ids_ref, *refs):
    part_refs, (grad_ref, memory_ref, own_ref, other_ref) = refs[:4], refs[4:]
    core = ids_ref[0]
    summed = mean_of(part_refs)
    tiled = jnp.concatenate([summed] * 4, axis=0)
    square = lax.dot_general(
        summed, tiled, (((1,), (1,)), ((), ())), precision=lax.Precision.HIGHEST, preferred_element_type=F32
    )
    lane = lax.broadcasted_iota(jnp.int32, (8, 128), 1) // 32
    gram = jnp.zeros((8, 128), F32)
    for group in range(4):
        gram = jnp.where(lane == group, square[8 * group : 8 * group + 8], gram)
    groups = [summed[8 * q : 8 * q + 8] for q in range(4)]
    even = core == 0
    ordered = jnp.concatenate(
        [
            jnp.where(even, groups[0], groups[1]),
            jnp.where(even, groups[2], groups[3]),
            jnp.where(even, groups[1], groups[0]),
            jnp.where(even, groups[3], groups[2]),
        ],
        axis=0,
    )
    left = jnp.concatenate(three_parts(ordered), axis=0).astype(BF16)
    left = jnp.concatenate([left, left], axis=1)

    @pl.loop(0, STEPS, unroll=2)
    def _(step):
        cols = pl.ds(pl.multiple_of(step * STEP_WIDTH, 128), STEP_WIDTH)
        both = jnp.concatenate([grad_ref[:, cols], memory_ref[:, cols]], axis=0)
        product = jnp.dot(left, both, preferred_element_type=F32)
        product = product[:32] + (product[32:64] + product[64:])
        for member in range(GROUP):
            chunk = step * GROUP + member
            for half, ref in enumerate((own_ref, other_ref)):
                for row in range(2):
                    base = 16 * half + 8 * row
                    for tile in range(TILES):
                        left_edge = WIDTH * member + 128 * tile
                        ref[chunk, row, tile] = product[base : base + 8, left_edge : left_edge + 128]
                    ref[chunk, row, TILES] = gram


def project(ids, parts, grad, memory):
    shape = jax.ShapeDtypeStruct((CHUNKS, 2, TILES + 1, 8, 128), F32)
    return pl.pallas_call(
        project_kernel,
        out_shape=(shape, shape),
        in_specs=[SMEM] + [VMEM] * 6,
        out_specs=(VMEM, VMEM),
        compiler_params=params(16 * MB),
        name="project",
    )(ids, *parts, grad, memory)


def factor_kernel(ids_ref, gram_ref, *refs):
    part_refs, (left_ref, inverse_ref, back_ref) = refs[:4], refs[4:]
    core = ids_ref[0]
    row = lax.broadcasted_iota(jnp.int32, (8, 128), 0)
    lane = lax.broadcasted_iota(jnp.int32, (8, 128), 1)
    tile = gram_ref[...] * (1.0 / 8)
    work, scales = [], []
    for q in range(4):
        part = pltpu.roll(tile, 128 - 32 * q, 1) if q else tile
        work.append(jnp.where(lane < 32, part, jnp.where(lane == row + (32 + 8 * q), 1.0, 0.0)))
    summed = mean_of(part_refs)
    basis = [summed[8 * q : 8 * q + 8] for q in range(4)]
    for p in range(4):
        below = range(p, 4)
        columns = [
            {g: jnp.broadcast_to(work[g][:, 8 * p + q : 8 * p + q + 1], (8, 128)) for g in below} for q in range(8)
        ]
        scale = jnp.ones((8, 128), F32)
        for q in range(8):
            pivot = columns[q][p][q : q + 1]
            scale = jnp.where(row == q, pivot, scale)
            ratio = 1.0 / pivot
            factors = {g: columns[q][g] * ratio for g in below}
            factors[p] = jnp.where(row > q, factors[p], 0.0)
            for later in range(q + 1, 8):
                edge = columns[later][p][q : q + 1]
                for g in below:
                    columns[later][g] = columns[later][g] - factors[g] * edge
            work_row, basis_row = work[p][q : q + 1], basis[p][q : q + 1]
            for g in below:
                work[g] = work[g] - factors[g] * work_row
                basis[g] = basis[g] - factors[g] * basis_row
        scales.append(lax.rsqrt(scale))
    scale = jnp.concatenate(scales, axis=0)
    work, basis = jnp.concatenate(work, axis=0), jnp.concatenate(basis, axis=0)
    lanes = lax.broadcasted_iota(jnp.int32, (RANK, 128), 1)
    left = basis * scale
    left_ref[...] = left
    inverse = pltpu.roll(work * scale, 96, 1)
    inverse = jnp.where(lanes < 32, inverse, 0.0)
    inverse_ref[...] = inverse
    solved = lax.dot_general(
        inverse, left, (((0,), (0,)), ((), ())), precision=lax.Precision.HIGHEST, preferred_element_type=F32
    )[:32] * (1.0 / 8)
    even = core == 0
    groups = [solved[8 * q : 8 * q + 8] for q in range(4)]
    ordered = jnp.concatenate(
        [
            jnp.where(even, groups[0], groups[1]),
            jnp.where(even, groups[2], groups[3]),
            jnp.where(even, groups[1], groups[0]),
            jnp.where(even, groups[3], groups[2]),
        ],
        axis=0,
    )
    one, two, three = three_parts(ordered)
    stack = jnp.concatenate([one, two, three, one, two, one, jnp.zeros((64, 128), F32)], axis=0)
    back_ref[...] = stack.T.astype(BF16)


def factor(ids, gram, parts):
    return pl.pallas_call(
        factor_kernel,
        out_shape=(
            jax.ShapeDtypeStruct((RANK, ROWS), F32),
            jax.ShapeDtypeStruct((RANK, 128), F32),
            jax.ShapeDtypeStruct((ROWS, 256), BF16),
        ),
        in_specs=[SMEM] + [VMEM] * 5,
        out_specs=(VMEM, VMEM, VMEM),
        compiler_params=params(16 * MB),
        cost_estimate=pl.CostEstimate(flops=2 * 10**10, bytes_accessed=10**7, transcendentals=0),
        name="factor",
    )(ids, gram, *parts)


def update_kernel(
    ids_ref, own_ref, other_ref, inverse_ref, back_ref, grad_ref, memory_ref,
    share_ref, out_hbm, out_ref, store_sems,
):
    def columns(step):
        return pl.ds(step * LAST_WIDTH, LAST_WIDTH)

    def store(step):
        cols = columns(step)
        return pltpu.make_async_copy(out_ref.at[:, cols], out_hbm.at[:, cols], store_sems.at[step])

    even = ids_ref[0] == 0
    back = back_ref[:, :192]

    def block(chunk, tile):
        parts = [ref[chunk, row, tile] for ref in (own_ref, other_ref) for row in range(2)]
        return jnp.concatenate(parts, axis=0)

    for step in range(LAST_STEPS):
        tiles = [block(step * LAST_GROUP + member, tile) for member in range(LAST_GROUP) for tile in range(TILES)]
        right = jnp.concatenate(tiles, axis=1)
        one, two, three = (part.astype(BF16) for part in three_parts(right))
        stack = jnp.concatenate([one, one, one, two, two, three], axis=0)
        update = jnp.dot(back, stack, preferred_element_type=F32)
        cols = columns(step)
        merged = grad_ref[:, cols].astype(F32) + memory_ref[:, cols].astype(F32)
        out_ref[:, cols] = (merged - update).astype(BF16)
        store(step).start()

    mine, odd = ids_ref[1], ids_ref[2]

    def natural(tile):
        own0, own1, other0, other1 = (ref[mine, row, tile] for ref in (own_ref, other_ref) for row in range(2))
        return jnp.concatenate(
            [
                jnp.where(even, own0, other0),
                jnp.where(even, other0, own0),
                jnp.where(even, own1, other1),
                jnp.where(even, other1, own1),
            ],
            axis=0,
        )

    right = jnp.concatenate([natural(tile) for tile in range(TILES)], axis=1)
    share = jnp.dot(
        inverse_ref[:, :32], right, precision=lax.Precision.HIGHEST, preferred_element_type=F32
    ) * (1.0 / 8)
    half = WIDTH // 2
    share_ref[...] = jnp.where(odd == 0, share[:, :half], share[:, half:])

    for step in range(LAST_STEPS):
        store(step).wait()


def finish(ids, own, other, inverse, back, grad, memory):
    return pl.pallas_call(
        update_kernel,
        out_shape=(
            jax.ShapeDtypeStruct((RANK, WIDTH // 2), F32),
            jax.ShapeDtypeStruct((ROWS, FF), BF16),
        ),
        in_specs=[SMEM] + [VMEM] * 6,
        out_specs=(VMEM, ANY),
        scratch_shapes=[pltpu.VMEM((ROWS, FF), BF16), pltpu.SemaphoreType.DMA((LAST_STEPS,))],
        compiler_params=params(16 * MB),
        name="finish",
    )(ids, own, other, inverse, back, grad, memory)


def exchange(value, axes):
    return lax.all_to_all(value, axes, 0, 0, tiled=True)


def swap(value):
    return lax.ppermute(value, "c", [(0, 1), (1, 0)])


def four(value, axes):
    three, two, one = (lax.ppermute(value, axes, [(i, i ^ k) for i in range(4)]) for k in (3, 2, 1))
    return value, one, two, three


def spread(value, axes, count):
    return exchange(jnp.broadcast_to(value[None], (count,) + value.shape), axes)


def resident(value):
    return pltpu.with_memory_space_constraint(value, pltpu.VMEM)


def far(value):
    return pltpu.with_memory_space_constraint(value, pltpu.HBM)


def on_device(gradients, residual, sketch):
    core = lax.axis_index("c")
    block = lax.axis_index(("x", "z4", "z2"))
    ids = jnp.stack([core, block, lax.axis_index("z1")]).astype(jnp.int32)
    far_grad = far(gradients[0])
    partial, grad = left_sketch(far_grad, residual[0], far(sketch))
    ids, partial = lax.optimization_barrier((ids, partial))
    pair = partial + swap(partial)
    parts = four(pair, "y")
    own, other = project(ids, parts, resident(grad), resident(residual[0]))
    terms = own + swap(other)
    terms = exchange(terms.reshape(32, TILES + 1, 8, 128), SPREAD)
    terms = jnp.sum(terms, axis=0)
    one, two, three, last = four(terms, ("z4", "z2"))
    terms = (one + two) + (three + last)
    gathered = spread(terms[:TILES], SPREAD, 32).reshape(CHUNKS, 2, TILES, 8, 128)
    gathered, gram = lax.optimization_barrier((gathered, terms[TILES]))
    left, inverse, back = factor(ids, gram, parts)
    share, fresh = finish(
        ids, gathered, swap(gathered), inverse, back, resident(gradients[0]), resident(residual[0])
    )
    return left, share, fresh[None]


def solution(mesh):
    fine = Mesh(mesh.devices.reshape(SIZES), AXES)
    outer, rep = ("y", "c"), ("x", "z4", "z2", "z1")
    return jax.shard_map(
        on_device,
        mesh=fine,
        in_specs=(P(outer, rep, None), P(outer, rep, None), P()),
        out_specs=(P(None, rep), P(None, rep), P(outer, rep, None)),
        check_vma=False,
    )
```

```python
import jax
import jax.numpy as jnp
from jax import lax
from jax.experimental import pallas as pl
from jax.experimental.pallas import tpu as pltpu
from jax.sharding import Mesh
from jax.sharding import PartitionSpec as P

AXES = ("y", "c", "x", "z4", "z2", "z1")
SIZES = (4, 2, 4, 2, 2, 2)
SPREAD = ("y", "x", "z1")
ROWS = 128
FF = 14336
RANK = 32
CHUNKS = 16
WIDTH = FF // CHUNKS
TILES = WIDTH // 128
LOADS = 8
LOAD_WIDTH = FF // LOADS
GROUP = 4
STEPS = CHUNKS // GROUP
STEP_WIDTH = GROUP * WIDTH
LAST_GROUP = 2
LAST_STEPS = CHUNKS // LAST_GROUP
LAST_WIDTH = LAST_GROUP * WIDTH
F32 = jnp.float32
BF16 = jnp.bfloat16
MB = 1024 * 1024

ANY = pl.BlockSpec(memory_space=pl.ANY)
VMEM = pl.BlockSpec(memory_space=pltpu.VMEM)
SMEM = pl.BlockSpec(memory_space=pltpu.SMEM)


def params(limit):
    return pltpu.CompilerParams(vmem_limit_bytes=limit)


def three_parts(value):
    first = value.astype(BF16).astype(F32)
    rest = value - first
    second = rest.astype(BF16).astype(F32)
    return first, second, rest - second


def product(sketch, block):
    return lax.dot_general(sketch, block, (((1,), (1,)), ((), ())), preferred_element_type=F32)


def first_kernel(grad_hbm, sketch_hbm, out_ref, grad_ref, sketch_ref, sems):
    copies = []
    for step in range(LOADS):
        cols = pl.ds(step * LOAD_WIDTH, LOAD_WIDTH)
        group = [
            pltpu.make_async_copy(src.at[:, cols], dst.at[:, cols], sems.at[step, which])
            for which, (src, dst) in enumerate(((sketch_hbm, sketch_ref), (grad_hbm, grad_ref)))
        ]
        for copy in group:
            copy.start()
        copies.append(group)
    total = jnp.zeros((RANK, ROWS), F32)
    for step in range(LOADS):
        for copy in copies[step]:
            copy.wait()
        cols = pl.ds(step * LOAD_WIDTH, LOAD_WIDTH)
        total += product(sketch_ref[:, cols], grad_ref[:, cols])
    out_ref[...] = total


def second_kernel(first_ref, sketch_ref, memory_ref, out_ref):
    out_ref[...] = first_ref[...] + product(sketch_ref[...], memory_ref[...])


def left_sketch(grad, memory, sketch):
    first, near_grad, near_sketch = pl.pallas_call(
        first_kernel,
        out_shape=(
            jax.ShapeDtypeStruct((RANK, ROWS), F32),
            pltpu.VMEM((ROWS, FF), BF16),
            pltpu.VMEM((RANK, FF), BF16),
        ),
        in_specs=[ANY, ANY],
        out_specs=(VMEM,) * 3,
        scratch_shapes=[pltpu.SemaphoreType.DMA((LOADS, 2))],
        compiler_params=params(16 * MB),
        cost_estimate=pl.CostEstimate(flops=2 * 10**10, bytes_accessed=10**7, transcendentals=0),
        name="left_first",
    )(grad, sketch)
    total = pl.pallas_call(
        second_kernel,
        out_shape=jax.ShapeDtypeStruct((RANK, ROWS), F32),
        in_specs=[VMEM] * 3,
        out_specs=VMEM,
        compiler_params=params(16 * MB),
        name="left_second",
    )(first, resident(near_sketch), resident(memory))
    return total, near_grad


def mean_of(part_refs):
    one, two, three, four = (ref[...] for ref in part_refs)
    return ((one + two) + (three + four)) * (1.0 / 8)


def project_kernel(ids_ref, *refs):
    part_refs, (grad_ref, memory_ref, own_ref, other_ref) = refs[:4], refs[4:]
    core = ids_ref[0]
    summed = mean_of(part_refs)
    tiled = jnp.concatenate([summed] * 4, axis=0)
    square = lax.dot_general(
        summed, tiled, (((1,), (1,)), ((), ())), precision=lax.Precision.HIGHEST, preferred_element_type=F32
    )
    lane = lax.broadcasted_iota(jnp.int32, (8, 128), 1) // 32
    gram = jnp.zeros((8, 128), F32)
    for group in range(4):
        gram = jnp.where(lane == group, square[8 * group : 8 * group + 8], gram)
    groups = [summed[8 * q : 8 * q + 8] for q in range(4)]
    even = core == 0
    ordered = jnp.concatenate(
        [
            jnp.where(even, groups[0], groups[1]),
            jnp.where(even, groups[2], groups[3]),
            jnp.where(even, groups[1], groups[0]),
            jnp.where(even, groups[3], groups[2]),
        ],
        axis=0,
    )
    left = jnp.concatenate(three_parts(ordered), axis=0).astype(BF16)
    left = jnp.concatenate([left, left], axis=1)

    @pl.loop(0, STEPS, unroll=4)
    def _(step):
        cols = pl.ds(pl.multiple_of(step * STEP_WIDTH, 128), STEP_WIDTH)
        both = jnp.concatenate([grad_ref[:, cols], memory_ref[:, cols]], axis=0)
        product = jnp.dot(left, both, preferred_element_type=F32)
        product = product[:32] + (product[32:64] + product[64:])
        for member in range(GROUP):
            chunk = step * GROUP + member
            for half, ref in enumerate((own_ref, other_ref)):
                for row in range(2):
                    base = 16 * half + 8 * row
                    for tile in range(TILES):
                        left_edge = WIDTH * member + 128 * tile
                        ref[chunk, row, tile] = product[base : base + 8, left_edge : left_edge + 128]
                    ref[chunk, row, TILES] = gram


def project(ids, parts, grad, memory):
    shape = jax.ShapeDtypeStruct((CHUNKS, 2, TILES + 1, 8, 128), F32)
    return pl.pallas_call(
        project_kernel,
        out_shape=(shape, shape),
        in_specs=[SMEM] + [VMEM] * 6,
        out_specs=(VMEM, VMEM),
        compiler_params=params(16 * MB),
        name="project",
    )(ids, *parts, grad, memory)


def factor_kernel(ids_ref, gram_ref, *refs):
    part_refs, (left_ref, inverse_ref, back_ref) = refs[:4], refs[4:]
    core = ids_ref[0]
    row = lax.broadcasted_iota(jnp.int32, (8, 128), 0)
    lane = lax.broadcasted_iota(jnp.int32, (8, 128), 1)
    tile = gram_ref[...] * (1.0 / 8)
    work, scales = [], []
    for q in range(4):
        part = pltpu.roll(tile, 128 - 32 * q, 1) if q else tile
        work.append(jnp.where(lane < 32, part, jnp.where(lane == row + (32 + 8 * q), 1.0, 0.0)))
    summed = mean_of(part_refs)
    basis = [summed[8 * q : 8 * q + 8] for q in range(4)]
    for p in range(4):
        below = range(p, 4)
        columns = [
            {g: jnp.broadcast_to(work[g][:, 8 * p + q : 8 * p + q + 1], (8, 128)) for g in below} for q in range(8)
        ]
        scale = jnp.ones((8, 128), F32)
        for q in range(8):
            pivot = columns[q][p][q : q + 1]
            scale = jnp.where(row == q, pivot, scale)
            ratio = 1.0 / pivot
            factors = {g: columns[q][g] * ratio for g in below}
            factors[p] = jnp.where(row > q, factors[p], 0.0)
            for later in range(q + 1, 8):
                edge = columns[later][p][q : q + 1]
                for g in below:
                    columns[later][g] = columns[later][g] - factors[g] * edge
            work_row, basis_row = work[p][q : q + 1], basis[p][q : q + 1]
            for g in below:
                work[g] = work[g] - factors[g] * work_row
                basis[g] = basis[g] - factors[g] * basis_row
        scales.append(lax.rsqrt(scale))
    scale = jnp.concatenate(scales, axis=0)
    work, basis = jnp.concatenate(work, axis=0), jnp.concatenate(basis, axis=0)
    lanes = lax.broadcasted_iota(jnp.int32, (RANK, 128), 1)
    left = basis * scale
    left_ref[...] = left
    inverse = pltpu.roll(work * scale, 96, 1)
    inverse = jnp.where(lanes < 32, inverse, 0.0)
    inverse_ref[...] = inverse
    solved = lax.dot_general(
        inverse, left, (((0,), (0,)), ((), ())), precision=lax.Precision.HIGHEST, preferred_element_type=F32
    )[:32] * (1.0 / 8)
    even = core == 0
    groups = [solved[8 * q : 8 * q + 8] for q in range(4)]
    ordered = jnp.concatenate(
        [
            jnp.where(even, groups[0], groups[1]),
            jnp.where(even, groups[2], groups[3]),
            jnp.where(even, groups[1], groups[0]),
            jnp.where(even, groups[3], groups[2]),
        ],
        axis=0,
    )
    one, two, three = three_parts(ordered)
    stack = jnp.concatenate([one, two, three, one, two, one, jnp.zeros((64, 128), F32)], axis=0)
    back_ref[...] = stack.T.astype(BF16)


def factor(ids, gram, parts):
    return pl.pallas_call(
        factor_kernel,
        out_shape=(
            jax.ShapeDtypeStruct((RANK, ROWS), F32),
            jax.ShapeDtypeStruct((RANK, 128), F32),
            jax.ShapeDtypeStruct((ROWS, 256), BF16),
        ),
        in_specs=[SMEM] + [VMEM] * 5,
        out_specs=(VMEM, VMEM, VMEM),
        compiler_params=params(16 * MB),
        cost_estimate=pl.CostEstimate(flops=2 * 10**10, bytes_accessed=10**7, transcendentals=0),
        name="factor",
    )(ids, gram, *parts)


def update_kernel(
    ids_ref, own_ref, other_ref, inverse_ref, back_ref, grad_ref, memory_ref,
    share_ref, out_hbm, out_ref, store_sems,
):
    def columns(step):
        return pl.ds(step * LAST_WIDTH, LAST_WIDTH)

    def store(step):
        cols = columns(step)
        return pltpu.make_async_copy(out_ref.at[:, cols], out_hbm.at[:, cols], store_sems.at[step])

    even = ids_ref[0] == 0
    back = back_ref[:, :192]

    def block(chunk, tile):
        parts = [ref[chunk, row, tile] for ref in (own_ref, other_ref) for row in range(2)]
        return jnp.concatenate(parts, axis=0)

    for step in range(LAST_STEPS):
        tiles = [block(step * LAST_GROUP + member, tile) for member in range(LAST_GROUP) for tile in range(TILES)]
        right = jnp.concatenate(tiles, axis=1)
        one, two, three = (part.astype(BF16) for part in three_parts(right))
        stack = jnp.concatenate([one, one, one, two, two, three], axis=0)
        update = jnp.dot(back, stack, preferred_element_type=F32)
        cols = columns(step)
        merged = grad_ref[:, cols].astype(F32) + memory_ref[:, cols].astype(F32)
        out_ref[:, cols] = (merged - update).astype(BF16)
        store(step).start()

    mine, odd = ids_ref[1], ids_ref[2]

    def natural(tile):
        own0, own1, other0, other1 = (ref[mine, row, tile] for ref in (own_ref, other_ref) for row in range(2))
        return jnp.concatenate(
            [
                jnp.where(even, own0, other0),
                jnp.where(even, other0, own0),
                jnp.where(even, own1, other1),
                jnp.where(even, other1, own1),
            ],
            axis=0,
        )

    right = jnp.concatenate([natural(tile) for tile in range(TILES)], axis=1)
    share = jnp.dot(
        inverse_ref[:, :32], right, precision=lax.Precision.HIGHEST, preferred_element_type=F32
    ) * (1.0 / 8)
    half = WIDTH // 2
    share_ref[...] = jnp.where(odd == 0, share[:, :half], share[:, half:])

    for step in range(LAST_STEPS):
        store(step).wait()


def finish(ids, own, other, inverse, back, grad, memory):
    return pl.pallas_call(
        update_kernel,
        out_shape=(
            jax.ShapeDtypeStruct((RANK, WIDTH // 2), F32),
            jax.ShapeDtypeStruct((ROWS, FF), BF16),
        ),
        in_specs=[SMEM] + [VMEM] * 6,
        out_specs=(VMEM, ANY),
        scratch_shapes=[pltpu.VMEM((ROWS, FF), BF16), pltpu.SemaphoreType.DMA((LAST_STEPS,))],
        compiler_params=params(16 * MB),
        name="finish",
    )(ids, own, other, inverse, back, grad, memory)


def exchange(value, axes):
    return lax.all_to_all(value, axes, 0, 0, tiled=True)


def swap(value):
    return lax.ppermute(value, "c", [(0, 1), (1, 0)])


def four(value, axes):
    three, two, one = (lax.ppermute(value, axes, [(i, i ^ k) for i in range(4)]) for k in (3, 2, 1))
    return value, one, two, three


def spread(value, axes, count):
    return exchange(jnp.broadcast_to(value[None], (count,) + value.shape), axes)


def resident(value):
    return pltpu.with_memory_space_constraint(value, pltpu.VMEM)


def far(value):
    return pltpu.with_memory_space_constraint(value, pltpu.HBM)


def on_device(gradients, residual, sketch):
    core = lax.axis_index("c")
    block = lax.axis_index(("x", "z4", "z2"))
    ids = jnp.stack([core, block, lax.axis_index("z1")]).astype(jnp.int32)
    far_grad = far(gradients[0])
    partial, grad = left_sketch(far_grad, residual[0], far(sketch))
    ids, partial = lax.optimization_barrier((ids, partial))
    pair = partial + swap(partial)
    parts = four(pair, "y")
    own, other = project(ids, parts, resident(grad), resident(residual[0]))
    terms = own + swap(other)
    terms = exchange(terms.reshape(32, TILES + 1, 8, 128), SPREAD)
    terms = jnp.sum(terms, axis=0)
    one, two, three, last = four(terms, ("z4", "z2"))
    terms = (one + two) + (three + last)
    gathered = spread(terms[:TILES], SPREAD, 32).reshape(CHUNKS, 2, TILES, 8, 128)
    gathered, gram = lax.optimization_barrier((gathered, terms[TILES]))
    left, inverse, back = factor(ids, gram, parts)
    share, fresh = finish(
        ids, gathered, swap(gathered), inverse, back, resident(gradients[0]), resident(residual[0])
    )
    return left, share, fresh[None]


def solution(mesh):
    fine = Mesh(mesh.devices.reshape(SIZES), AXES)
    outer, rep = ("y", "c"), ("x", "z4", "z2", "z1")
    return jax.shard_map(
        on_device,
        mesh=fine,
        in_specs=(P(outer, rep, None), P(outer, rep, None), P()),
        out_specs=(P(None, rep), P(None, rep), P(outer, rep, None)),
        check_vma=False,
    )
```
